32 devices in a mesh: dp: 32 (over z, y, x, core), tensor: 1.
Axes of the slice: x: 2, y: 2, z: 4, core: 2. Of those that a mesh axis runs over, the one named last changes fastest.
Arguments:
- tokens: bfloat16 [4096, 14336], P('dp', 'tensor'), may hold values from -22 to 22
- frozen_matrix: bfloat16 [14336, 4096], P('tensor', 'dp')
- adapter_down_factor: bfloat16 [14336, 64], P('tensor'), may hold values from -0.046875 to 0.046875
- adapter_up_factor: bfloat16 [64, 4096], P(None, 'tensor'), may hold values from -3 to 3
- magnitude: bfloat16 [4096], P('tensor'), may hold values from 0.5 to 2
- cotangent: bfloat16 [4096, 4096], P('dp'), may hold values from -6 to 6
Outputs:
- output: bfloat16 [4096, 4096], P('dp', 'tensor')
- input_gradient: bfloat16 [4096, 14336], P('dp', 'tensor')
- grad_down: float32 [14336, 64], P('tensor')
- grad_up: float32 [64, 4096], P(None, 'tensor')
- grad_magnitude: float32 [4096], P('tensor')
The draws below stay inside these ranges and needn't reach their ends.
All inputs are finite; a program needn't handle non-finite values.
Results may differ from the reference program's by a relative error of at most 0.0056.
Values may be sent and summed in bfloat16 or wider, within the bound.
A program may use at most 192 MiB of HBM per device.

```python
import math
import jax
import jax.numpy as jnp
from jax import lax

OUTPUT_FEATURES = 4096
INPUT_FEATURES = 14336
ADAPTER_RANK = 64
TOKENS = 4096


def draw_tokens(key, part):
    key = jax.random.fold_in(key, 11)
    first, second = jax.random.split(key)
    values = jnp.clip(jax.random.normal(first, (TOKENS, INPUT_FEATURES), jnp.float32), -4.0, 4.0)
    trend = 3.0
    spread = jax.random.uniform(second, (TOKENS, 1), jnp.float32)
    position = jnp.arange(TOKENS, dtype=jnp.float32)[:, None] / max(TOKENS - 1, 1)
    row_scale = jnp.power(10.0, spread - 0.5) * jnp.power(trend, position - 0.5)
    return (values * row_scale).astype(jnp.bfloat16)


def draw_frozen_matrix(key, part):
    key = jax.random.fold_in(key, 23)
    first, second, third = jax.random.split(key, 3)
    values = jnp.clip(jax.random.normal(first, (INPUT_FEATURES, OUTPUT_FEATURES), jnp.float32), -4.0, 4.0)
    trend = 3.0
    row_spread = jax.random.uniform(second, (INPUT_FEATURES, 1), jnp.float32)
    column_spread = jax.random.uniform(third, (1, OUTPUT_FEATURES), jnp.float32)
    position = jnp.arange(INPUT_FEATURES, dtype=jnp.float32)[:, None] / max(INPUT_FEATURES - 1, 1)
    row_scale = jnp.power(10.0, row_spread - 0.5) * jnp.power(trend, position - 0.5)
    column_scale = jnp.power(10.0, column_spread - 0.5)
    return (values * row_scale * column_scale / jnp.sqrt(jnp.float32(INPUT_FEATURES))).astype(jnp.bfloat16)


def shard_levels(own_key, extent, cuts, smallest, largest):
    def one(dim, blocks):
        steps = jax.random.uniform(jax.random.fold_in(jax.random.fold_in(own_key, 6), dim), (blocks,), jnp.float32, smallest / len(cuts), largest / len(cuts))
        return jnp.repeat(jnp.exp(steps), extent[dim] // blocks).reshape((-1,) + (1,) * (len(extent) - dim - 1))

    factor_of = one(*cuts[0])
    for cut in cuts[1:]:
        factor_of = factor_of * one(*cut)
    return factor_of


def centred(key, extent, width, bound, cuts=(), kind=jnp.bfloat16):
    array = jax.random.normal(key, extent, jnp.float32) * width
    if len(cuts) > 0:
        array = shard_levels(key, extent, cuts, -0.22, 0.18) * array
    return jnp.clip(array, min=-bound, max=bound).astype(kind)


def setup_inputs(seed: int = 0) -> dict:
    keys = jax.random.split(jax.random.key(seed), 7)
    return {
        "tokens": draw_tokens(jax.random.fold_in(keys[6], 71), 0),
        "frozen_matrix": draw_frozen_matrix(jax.random.fold_in(keys[6], 71), 0),
        "adapter_down_factor": centred(keys[2], (INPUT_FEATURES, ADAPTER_RANK), INPUT_FEATURES ** -0.5, 0.046875),
        "adapter_up_factor": centred(keys[3], (ADAPTER_RANK, OUTPUT_FEATURES), 4 ** -0.5, 3.0),
        "magnitude": jnp.clip(jnp.exp(jax.random.uniform(keys[4], (OUTPUT_FEATURES,), jnp.float32, math.log(0.5), math.log(2.0))), 0.5, 2.0).astype(jnp.bfloat16),
        "cotangent": centred(keys[5], (TOKENS, OUTPUT_FEATURES), 1.0, 6.0, ((0, 32),)),
    }


epsilon = 1e-06

def reference(tokens, frozen_matrix, adapter_down_factor, adapter_up_factor, magnitude, cotangent):
    rank_activation = jnp.dot(tokens, adapter_down_factor, preferred_element_type=jnp.float32).astype(jnp.bfloat16)
    combined_output = frozen_matrix.astype(jnp.float32) + jnp.dot(adapter_down_factor, adapter_up_factor, preferred_element_type=jnp.float32)
    squares = lax.optimization_barrier(jnp.sum(combined_output * combined_output, axis=0))
    norm = jnp.sqrt(squares + epsilon)
    scale = magnitude.astype(jnp.float32) / norm
    frozen_output = jnp.dot(tokens, frozen_matrix, preferred_element_type=jnp.float32)
    merged_weight = frozen_output + jnp.dot(rank_activation, adapter_up_factor, preferred_element_type=jnp.float32)
    output = (merged_weight * scale).astype(jnp.bfloat16)
    rescaled_gradient = (cotangent.astype(jnp.float32) * scale).astype(jnp.bfloat16)
    rank_gradient = jnp.dot(rescaled_gradient, adapter_up_factor.T, preferred_element_type=jnp.float32).astype(jnp.bfloat16)
    input_gradient = jnp.dot(rescaled_gradient, frozen_matrix.T, preferred_element_type=jnp.float32)
    input_gradient = (input_gradient + jnp.dot(rank_gradient, adapter_down_factor.T, preferred_element_type=jnp.float32)).astype(jnp.bfloat16)
    factor = 1.0 / jnp.sqrt(jnp.float32(TOKENS))
    grad_down = jnp.dot(tokens.T, rank_gradient, preferred_element_type=jnp.float32) * factor
    grad_up = jnp.dot(rank_activation.T, rescaled_gradient, preferred_element_type=jnp.float32) * factor
    grad_magnitude = lax.optimization_barrier(jnp.sum(cotangent.astype(jnp.float32) * merged_weight / norm, axis=0)) * factor
    return (output, input_gradient, grad_down, grad_up, grad_magnitude)
```

```python
import functools
import math

import jax
import jax.numpy as jnp
from jax import lax
from jax.experimental import pallas as pl
from jax.experimental.pallas import tpu as pltpu
from jax.sharding import PartitionSpec as P

epsilon = 1e-06

CHIPS = 4
CORES = 2
PLANE = CHIPS * CORES


def place():
    me = lax.axis_index("dp")
    return me // PLANE, (me % PLANE) // CORES, me % CORES


def exchange_kernel(views, count, *refs):
    sources, targets = refs[:count], refs[count : 2 * count]
    send_sem, recv_sem, local_sem = refs[2 * count :]
    me = lax.axis_index("dp")
    chip = (me % PLANE) // CORES
    base = me - chip * CORES
    barrier = pltpu.get_barrier_semaphore()
    for hop in range(1, CHIPS):
        pl.semaphore_signal(
            barrier, inc=1, device_id={"dp": base + ((chip + hop) % CHIPS) * CORES},
            device_id_type=pl.DeviceIdType.MESH,
        )
    pl.semaphore_wait(barrier, CHIPS - 1)
    copies = []
    for number, view in enumerate(views):
        for hop in (2, 1, 3):
            other = (chip + hop) % CHIPS
            source, target = view(sources[number], targets[number], other, chip)
            copies.append(
                pltpu.make_async_remote_copy(
                    src_ref=source, dst_ref=target,
                    send_sem=send_sem.at[number, hop], recv_sem=recv_sem.at[number, hop],
                    device_id={"dp": base + other * CORES},
                    device_id_type=pl.DeviceIdType.MESH,
                )
            )
            copies[-1].start()
    for number, view in enumerate(views):
        source, target = view(sources[number], targets[number], chip, chip)
        copies.append(pltpu.make_async_copy(source, target, local_sem.at[number]))
        copies[-1].start()
    for copy in copies:
        copy.wait()


def exchange(views, sources, shapes, collective_id):
    count = len(views)
    moved = sum(math.prod(s.shape) * s.dtype.itemsize for s in shapes)
    return pl.pallas_call(
        functools.partial(exchange_kernel, views, count),
        out_shape=list(shapes),
        in_specs=[pl.BlockSpec(memory_space=pl.ANY)] * count,
        out_specs=[pl.BlockSpec(memory_space=pl.ANY)] * count,
        scratch_shapes=[
            pltpu.SemaphoreType.DMA((count, CHIPS)),
            pltpu.SemaphoreType.DMA((count, CHIPS)),
            pltpu.SemaphoreType.DMA((count,)),
        ],
        compiler_params=pltpu.CompilerParams(
            collective_id=collective_id, has_side_effects=True
        ),
        cost_estimate=pl.CostEstimate(flops=0, bytes_accessed=40 * moved, transcendentals=0),
    )(*sources)


def rows_to_columns(depth):
    def view(source, target, other, chip):
        rows = source.shape[0]
        return (
            source.at[:, pl.ds(pl.multiple_of(other * depth, 128), depth)],
            target.at[pl.ds(pl.multiple_of(chip * rows, 128), rows), :],
        )
    return view


def columns_to_rows(rows, depth):
    def view(source, target, other, chip):
        return (
            source.at[pl.ds(pl.multiple_of(other * rows, 128), rows), :],
            target.at[:, pl.ds(pl.multiple_of(chip * depth, 128), depth)],
        )
    return view


def whole_rows(source, target, other, chip):
    rows = source.shape[0]
    return source, target.at[pl.ds(pl.multiple_of(chip * rows, 128), rows), :]


def rows_to_slots(rows):
    def view(source, target, other, chip):
        return source.at[pl.ds(pl.multiple_of(other * rows, 128), rows), :], target.at[chip]
    return view


def frozen_view(depth, width):
    def view(source, target, other, chip):
        return (
            source.at[pl.ds(pl.multiple_of(other * depth, 128), depth), :],
            target.at[chip // 2, :, pl.ds(pl.multiple_of((chip % 2) * width, 128), width)],
        )
    return view


def dot(a, b, contract):
    return lax.dot_general(a, b, ((contract[:1], contract[1:]), ((), ())),
                           preferred_element_type=jnp.float32)


def on_plane(tokens, frozen, down, up, magnitude, cotangent):
    rows, features = tokens.shape
    width = frozen.shape[1]
    outputs = cotangent.shape[1]
    size = lax.axis_size("dp")
    planes = size // PLANE
    depth = features // CHIPS
    half = outputs // planes // 2
    me = lax.axis_index("dp")
    plane, chip, core = place()
    f32, bf16 = jnp.float32, jnp.bfloat16

    (blocks,) = exchange(
        [frozen_view(depth, width)], [frozen],
        [jax.ShapeDtypeStruct((2, depth, 2 * width), bf16)], 1,
    )
    blocks, tokens, frozen, cotangent = lax.optimization_barrier(
        (blocks, tokens, frozen, cotangent)
    )

    forward = [(i, (i + PLANE) % size) for i in range(size)]
    backward = [((i + PLANE) % size, i) for i in range(size)]
    across = [(i, i - i % CORES + (i + 1) % CORES) for i in range(size)]
    pieces = [[blocks[0], blocks[1]]]
    for step in range(planes - 1):
        pieces.append([
            lax.ppermute(pieces[-1][0], "dp", forward),
            lax.ppermute(pieces[-1][1], "dp", backward),
        ])
    others = [[lax.ppermute(part, "dp", across) for part in pair] for pair in pieces]

    tokens_part, cotangent_part = exchange(
        [rows_to_columns(depth), whole_rows], [tokens, cotangent],
        [jax.ShapeDtypeStruct((CHIPS * rows, depth), bf16),
         jax.ShapeDtypeStruct((CHIPS * rows, outputs), bf16)], 2,
    )

    own_up = lax.dynamic_slice_in_dim(up, me * width, width, 1)
    combined = frozen.astype(f32) + jnp.dot(down, own_up, preferred_element_type=f32)
    squares = lax.all_gather(jnp.sum(combined * combined, axis=0), "dp", axis=0, tiled=True)
    norm = jnp.sqrt(squares + epsilon)
    scale = magnitude.astype(f32) / norm

    rank_act = jnp.dot(tokens, down, preferred_element_type=f32).astype(bf16)
    adapter = jnp.dot(rank_act, up, preferred_element_type=f32)
    cot_own = cotangent.astype(f32)
    grad_own = (cot_own * scale).astype(bf16)
    back_own = dot(grad_own, up, (1, 1)).astype(bf16)
    factor = 1.0 / math.sqrt(rows * size)
    down_part = dot(tokens, back_own, (0, 0))
    up_part = dot(rank_act, grad_own, (0, 0))
    grad_down, grad_up = lax.psum((down_part, up_part), "dp")

    grad_part = (cotangent_part.astype(f32) * scale).astype(bf16)
    back_part = dot(grad_part, up, (1, 1)).astype(bf16)
    down_rows = lax.dynamic_slice_in_dim(down, chip * depth, depth, 0)
    gradient = dot(back_part, down_rows, (1, 1))

    partial, sums = [], []
    for step in range(planes):
        for side in range(2):
            where = (plane + (planes - step if side == 0 else step)) % planes
            start = where * 2 * half + side * half
            group = (CHIPS * rows, 2, CORES, width)
            cot = lax.dynamic_slice_in_dim(cotangent_part, start, half, 1)
            grad = lax.dynamic_slice_in_dim(grad_part, start, half, 1).reshape(group)
            outs = []
            for part, kind in ((pieces[step][side], core), (others[step][side], 1 - core)):
                outs.append(dot(tokens_part, part, (1, 0)))
                grad_kind = lax.dynamic_index_in_dim(grad, kind, 2, False)
                grad_kind = grad_kind.reshape(CHIPS * rows, 2 * width)
                gradient = gradient + dot(grad_kind, part, (1, 1))
            first = jnp.where(core == 0, outs[0], outs[1]).reshape(CHIPS * rows, 2, 1, width)
            second = jnp.where(core == 0, outs[1], outs[0]).reshape(CHIPS * rows, 2, 1, width)
            out = jnp.concatenate([first, second], axis=2).reshape(CHIPS * rows, half)
            sums.append(jnp.sum(cot.astype(f32) * out, axis=0))
            partial.append(out.astype(bf16))

    early = jnp.concatenate(partial[:-2], axis=1)
    late = jnp.concatenate(partial[-2:], axis=1)
    (early_slots,) = exchange(
        [rows_to_slots(rows)], [early],
        [jax.ShapeDtypeStruct((CHIPS, rows, early.shape[1]), bf16)], 3,
    )
    late_slots, input_gradient = exchange(
        [rows_to_slots(rows), columns_to_rows(rows, depth)], [late, gradient.astype(bf16)],
        [jax.ShapeDtypeStruct((CHIPS, rows, late.shape[1]), bf16),
         jax.ShapeDtypeStruct((rows, features), bf16)], 4,
    )

    def in_order(steps):
        lead = steps.shape[:-1]
        steps = steps.reshape(lead + (planes, 2, half))
        number = jnp.arange(planes)
        falling = jnp.take(steps[..., 0, :], (plane - number) % planes, axis=-2)
        rising = jnp.take(steps[..., 1, :], (number - plane) % planes, axis=-2)
        return jnp.stack([falling, rising], axis=-2).reshape(lead + (outputs,))

    sums = in_order(jnp.concatenate(sums)) + jnp.sum(cot_own * adapter, axis=0)
    grad_magnitude = jnp.sum(lax.all_gather(sums / norm, "dp"), axis=0)

    base = jnp.concatenate(
        [jnp.sum(early_slots.astype(f32), axis=0), jnp.sum(late_slots.astype(f32), axis=0)], axis=1
    )
    output = ((in_order(base) + adapter) * scale).astype(bf16)
    return (output, input_gradient, grad_down * factor, grad_up * factor, grad_magnitude * factor)


def on_device(tokens, frozen_matrix, adapter_down_factor, adapter_up_factor, magnitude, cotangent):
    tok_rows = tokens.shape[0]
    local_portion = adapter_up_factor.shape[1]
    gathered_up_factor, full_magnitude = (
        lax.all_gather(adapter_up_factor, "tensor", axis=1, tiled=True),
        lax.all_gather(magnitude, "tensor", axis=0, tiled=True),
    )
    rank_partial = jnp.dot(tokens, adapter_down_factor, preferred_element_type=jnp.float32)
    rank_activation = lax.psum(rank_partial, "tensor").astype(jnp.bfloat16)
    piece = lax.all_gather(frozen_matrix, "dp", axis=1, tiled=True)
    result = jnp.dot(tokens, piece, preferred_element_type=jnp.float32)
    combined_output = piece.astype(jnp.float32) + jnp.dot(
        adapter_down_factor, gathered_up_factor, preferred_element_type=jnp.float32
    )
    squares = jnp.sum(combined_output * combined_output, axis=0)
    square_part = squares
    squares = lax.psum(square_part, "tensor")
    norm = jnp.sqrt(squares + epsilon)
    scale = full_magnitude.astype(jnp.float32) / norm
    frozen_output = lax.psum_scatter(result, "tensor", scatter_dimension=1, tiled=True)
    shard_start = lax.axis_index("tensor") * local_portion
    merged_weight = frozen_output + jnp.dot(
        rank_activation, adapter_up_factor, preferred_element_type=jnp.float32
    )
    own_scale = lax.dynamic_slice_in_dim(scale, shard_start, local_portion, 0)
    own_norm_vals = lax.dynamic_slice_in_dim(norm, shard_start, local_portion, 0)
    output = (merged_weight * own_scale).astype(jnp.bfloat16)
    rescaled_gradient = (cotangent.astype(jnp.float32) * scale).astype(jnp.bfloat16)
    rank_gradient = jnp.dot(
        rescaled_gradient, gathered_up_factor.T, preferred_element_type=jnp.float32
    ).astype(jnp.bfloat16)
    gradient_running_total = lax.dot_general(
        rescaled_gradient,
        lax.all_gather(frozen_matrix, "dp", axis=1, tiled=True),
        (((1,), (1,)), ((), ())),
        preferred_element_type=jnp.float32,
    )
    input_gradient = (
        gradient_running_total
        + jnp.dot(rank_gradient, adapter_down_factor.T, preferred_element_type=jnp.float32)
    ).astype(jnp.bfloat16)
    own_grad = lax.dynamic_slice_in_dim(rescaled_gradient, shard_start, local_portion, 1)
    own_cotangent = lax.dynamic_slice_in_dim(cotangent, shard_start, local_portion, 1).astype(
        jnp.float32
    )
    down_part = lax.dot_general(
        tokens, rank_gradient, (((0,), (0,)), ((), ())), preferred_element_type=jnp.float32
    )
    up_part = lax.dot_general(
        rank_activation, own_grad, (((0,), (0,)), ((), ())), preferred_element_type=jnp.float32
    )
    magnitude_part = jnp.sum(own_cotangent * merged_weight / own_norm_vals, axis=0)
    grad_down, grad_up, grad_magnitude = lax.psum((down_part, up_part, magnitude_part), "dp")
    factor = 1.0 / math.sqrt(tok_rows * lax.axis_size("dp"))
    return (output, input_gradient, grad_down * factor, grad_up * factor, grad_magnitude * factor)


def solution(mesh):
    planes = mesh.shape["dp"] // PLANE
    in_planes = mesh.shape["tensor"] == 1 and mesh.shape["dp"] == PLANE * planes and planes > 1
    return jax.shard_map(
        on_plane if in_planes else on_device,
        mesh=mesh,
        in_specs=(
            P("dp", "tensor"),
            P("tensor", "dp"),
            P("tensor", None),
            P(None, "tensor"),
            P("tensor"),
            P("dp", None),
        ),
        out_specs=(
            P("dp", "tensor"),
            P("dp", "tensor"),
            P("tensor", None),
            P(None, "tensor"),
            P("tensor"),
        ),
        check_vma=False,
    )
```

```python
import functools
import math

import jax
import jax.numpy as jnp
from jax import lax
from jax.experimental import pallas as pl
from jax.experimental.pallas import tpu as pltpu
from jax.sharding import PartitionSpec as P

epsilon = 1e-06

CHIPS = 4
CORES = 2
PLANE = CHIPS * CORES


def place():
    me = lax.axis_index("dp")
    return me // PLANE, (me % PLANE) // CORES, me % CORES


def exchange_kernel(views, vector, *refs):
    count = len(views)
    ends = count + (vector is not None)
    sources, targets = refs[:count], refs[ends : ends + count]
    small_in, small_out = refs[ends - 1], refs[2 * ends - 1]
    scratch = refs[2 * ends :]
    send_sem, recv_sem, local_sem = scratch[:3]
    me = lax.axis_index("dp")
    planes = lax.axis_size("dp") // PLANE
    plane, chip, core = place()
    spot = me % PLANE
    base = me - chip * CORES

    def remote(source, target, send, recv, device):
        return pltpu.make_async_remote_copy(
            src_ref=source, dst_ref=target, send_sem=send, recv_sem=recv,
            device_id={"dp": device}, device_id_type=pl.DeviceIdType.MESH,
        )

    if vector is None:
        partners = [base + ((chip + hop) % CHIPS) * CORES for hop in range(1, CHIPS)]
    else:
        above = [(plane + hop) % planes * PLANE + spot for hop in range(1, planes)]
        beside = [plane * PLANE + (spot + hop) % PLANE for hop in range(1, PLANE)]
        partners = above + beside
    barrier = pltpu.get_barrier_semaphore()
    for device in partners:
        pl.semaphore_signal(
            barrier, inc=1, device_id={"dp": device}, device_id_type=pl.DeviceIdType.MESH
        )
    pl.semaphore_wait(barrier, len(partners))

    line = []
    if vector is not None:
        line_send, line_recv, flat_send, flat_recv = scratch[3:7]
        if vector == "gather":
            own = small_out.at[spot, plane]
            keep = pltpu.make_async_copy(small_in, own, local_sem.at[count])
            keep.start()
            start = small_in
        else:
            line_sum, flat_sum = scratch[7:9]
            own = line_sum.at[plane]
            own[...] = small_in[...]
            start = own
        for hop, device in enumerate(above):
            line.append(remote(start, own, line_send.at[hop], line_recv.at[hop], device))
            line[-1].start()
    copies = []
    for number, view in enumerate(views):
        for hop in (2, 1, 3):
            other = (chip + hop) % CHIPS
            source, target = view(sources[number], targets[number], other, chip)
            copies.append(remote(source, target, send_sem.at[number, hop],
                                 recv_sem.at[number, hop], base + other * CORES))
            copies[-1].start()
    for number, view in enumerate(views):
        source, target = view(sources[number], targets[number], chip, chip)
        copies.append(pltpu.make_async_copy(source, target, local_sem.at[number]))
        copies[-1].start()
    if vector is not None:
        for copy in line:
            copy.wait()
        if vector == "gather":
            keep.wait()
            block = small_out.at[spot]
        else:
            block = flat_sum.at[spot]
            block[...] = functools.reduce(lambda x, y: x + y, [line_sum[i] for i in range(planes)])
        for hop, device in enumerate(beside):
            copies.append(remote(block, block, flat_send.at[hop], flat_recv.at[hop], device))
            copies[-1].start()
    for copy in copies:
        copy.wait()
    if vector == "sum":
        small_out[...] = functools.reduce(lambda x, y: x + y, [flat_sum[i] for i in range(PLANE)])


def exchange(views, sources, shapes, collective_id, vector=None, small=None):
    count = len(views)
    planes = lax.axis_size("dp") // PLANE
    moved = sum(math.prod(s.shape) * s.dtype.itemsize for s in shapes)
    sources, shapes = list(sources), list(shapes)
    specs = [pl.BlockSpec(memory_space=pl.ANY)] * count
    dma = pltpu.SemaphoreType.DMA
    scratch = [dma((count, CHIPS)), dma((count, CHIPS)), dma((count + 1,))]
    if vector is not None:
        sources.append(small)
        scratch += [dma((planes,)), dma((planes,)), dma((PLANE,)), dma((PLANE,))]
        if vector == "gather":
            specs = specs + [pl.BlockSpec(memory_space=pl.ANY)]
            shapes.append(jax.ShapeDtypeStruct((PLANE, planes) + small.shape, small.dtype))
        else:
            specs = specs + [pl.BlockSpec(memory_space=pltpu.VMEM)]
            shapes.append(jax.ShapeDtypeStruct(small.shape, small.dtype))
            scratch += [pltpu.VMEM((planes,) + small.shape, small.dtype),
                        pltpu.VMEM((PLANE,) + small.shape, small.dtype)]
    return pl.pallas_call(
        functools.partial(exchange_kernel, views, vector),
        out_shape=shapes,
        in_specs=specs,
        out_specs=specs,
        scratch_shapes=scratch,
        compiler_params=pltpu.CompilerParams(
            collective_id=collective_id, has_side_effects=True
        ),
        cost_estimate=pl.CostEstimate(flops=0, bytes_accessed=40 * moved, transcendentals=0),
    )(*sources)


def to_arrival(info, x_ref, y_ref):
    width = x_ref.shape[1] // 4
    core = info[1]
    x = [x_ref[:, i * width : (i + 1) * width] for i in range(4)]
    for i, (zero, one) in enumerate(((0, 1), (2, 3), (1, 0), (3, 2))):
        y_ref[:, i * width : (i + 1) * width] = jnp.where(core == 0, x[zero], x[one])


def from_arrival(info, x_ref, y_ref):
    width = x_ref.shape[1] // 4
    core = info[1]
    x = [x_ref[:, i * width : (i + 1) * width] for i in range(4)]
    for i, (zero, one) in enumerate(((0, 2), (2, 0), (1, 3), (3, 1))):
        y_ref[:, i * width : (i + 1) * width] = jnp.where(core == 0, x[zero], x[one])


def finish_block(info, x_ref, adapter_ref, scale_ref, y_ref, base_ref):
    from_arrival(info, x_ref, base_ref)
    y_ref[...] = ((base_ref[...] + adapter_ref[...]) * scale_ref[...]).astype(y_ref.dtype)


def reorder(kernel, arrays, kind, forward, info, planes, scratch=()):
    rows, outputs = arrays[0].shape
    block = outputs // planes // 2

    def there(i, info):
        number, side, plane = i // 2, i % 2, info[0]
        falling = (plane + planes - number) % planes
        rising = (plane + number) % planes if forward else (number + planes - plane) % planes
        return 0, jnp.where(side == 0, falling, rising) * 2 + side

    def here(i, info):
        return 0, i

    specs = [pl.BlockSpec((rows, block), there)]
    specs += [pl.BlockSpec((a.shape[0], block), here) for a in arrays[1:]]
    return pl.pallas_call(
        kernel,
        out_shape=jax.ShapeDtypeStruct((rows, outputs), kind),
        grid_spec=pltpu.PrefetchScalarGridSpec(
            num_scalar_prefetch=1,
            grid=(planes * 2,),
            in_specs=specs,
            out_specs=pl.BlockSpec((rows, block), here),
            scratch_shapes=list(scratch),
        ),
    )(info, *arrays)


def rows_to_columns(depth):
    def view(source, target, other, chip):
        rows = source.shape[0]
        return (
            source.at[:, pl.ds(pl.multiple_of(other * depth, 128), depth)],
            target.at[pl.ds(pl.multiple_of(chip * rows, 128), rows), :],
        )
    return view


def columns_to_rows(rows, depth):
    def view(source, target, other, chip):
        return (
            source.at[pl.ds(pl.multiple_of(other * rows, 128), rows), :],
            target.at[:, pl.ds(pl.multiple_of(chip * depth, 128), depth)],
        )
    return view


def whole_rows(source, target, other, chip):
    rows = source.shape[0]
    return source, target.at[pl.ds(pl.multiple_of(chip * rows, 128), rows), :]


def rows_to_slots(rows):
    def view(source, target, other, chip):
        return source.at[pl.ds(pl.multiple_of(other * rows, 128), rows), :], target.at[chip]
    return view


def frozen_view(depth, width):
    def view(source, target, other, chip):
        return (
            source.at[pl.ds(pl.multiple_of(other * depth, 128), depth), :],
            target.at[chip // 2, :, pl.ds(pl.multiple_of((chip % 2) * width, 128), width)],
        )
    return view


def dot(a, b, contract):
    return lax.dot_general(a, b, ((contract[:1], contract[1:]), ((), ())),
                           preferred_element_type=jnp.float32)


def on_plane(tokens, frozen, down, up, magnitude, cotangent):
    rows, features = tokens.shape
    width = frozen.shape[1]
    outputs = cotangent.shape[1]
    size = lax.axis_size("dp")
    planes = size // PLANE
    depth = features // CHIPS
    block = outputs // planes
    me = lax.axis_index("dp")
    plane, chip, core = place()
    info = jnp.stack([plane, core]).astype(jnp.int32)
    f32, bf16 = jnp.float32, jnp.bfloat16

    own_up = lax.dynamic_slice_in_dim(up, me * width, width, 1)
    combined = frozen.astype(f32) + jnp.dot(down, own_up, preferred_element_type=f32)
    squares = jnp.broadcast_to(jnp.sum(combined * combined, axis=0)[None], (8, width))
    blocks, squares = exchange(
        [frozen_view(depth, width)], [frozen],
        [jax.ShapeDtypeStruct((2, depth, 2 * width), bf16)], 1, "gather", squares,
    )
    blocks, squares, tokens, cotangent = lax.optimization_barrier(
        (blocks, squares, tokens, cotangent)
    )

    forward = [(i, (i + PLANE) % size) for i in range(size)]
    backward = [((i + PLANE) % size, i) for i in range(size)]
    across = [(i, i - i % CORES + (i + 1) % CORES) for i in range(size)]
    pieces = [[blocks[0], blocks[1]]]
    for step in range(planes - 1):
        pieces.append([
            lax.ppermute(pieces[-1][0], "dp", forward),
            lax.ppermute(pieces[-1][1], "dp", backward),
        ])
    others = [[lax.ppermute(part, "dp", across) for part in pair] for pair in pieces]

    tokens_part, cotangent_part = exchange(
        [rows_to_columns(depth), whole_rows],
        [tokens, reorder(to_arrival, [cotangent], bf16, True, info, planes)],
        [jax.ShapeDtypeStruct((CHIPS * rows, depth), bf16),
         jax.ShapeDtypeStruct((CHIPS * rows, outputs), bf16)], 2,
    )

    norm = jnp.sqrt(squares[:, :, 0, :].transpose(1, 0, 2).reshape(outputs) + epsilon)
    scale = magnitude.astype(f32) / norm
    scale_rows = jnp.broadcast_to(scale[None], (8, outputs))
    scale_arrival = reorder(to_arrival, [scale_rows], f32, True, info, planes)[:1]

    rank_act = jnp.dot(tokens, down, preferred_element_type=f32).astype(bf16)
    adapter = jnp.dot(rank_act, up, preferred_element_type=f32)
    cot_own = cotangent.astype(f32)
    grad_own = (cot_own * scale).astype(bf16)
    back_own = dot(grad_own, up, (1, 1)).astype(bf16)
    factor = 1.0 / math.sqrt(rows * size)
    down_part = dot(tokens, back_own, (0, 0))
    up_part = dot(rank_act, grad_own, (0, 0))
    grad_down, grad_up = lax.psum((down_part, up_part), "dp")

    grad_part = (cotangent_part.astype(f32) * scale_arrival).astype(bf16)
    up_arrival = reorder(to_arrival, [up], bf16, True, info, planes)
    back_part = dot(grad_part, up_arrival, (1, 1)).astype(bf16)
    down_rows = lax.dynamic_slice_in_dim(down, chip * depth, depth, 0)
    gradient = dot(back_part, down_rows, (1, 1))

    partial, sums = [], []
    for step in range(planes):
        weight = jnp.concatenate(
            [pieces[step][0], others[step][0], pieces[step][1], others[step][1]], axis=1
        )
        columns = slice(step * block, (step + 1) * block)
        out = dot(tokens_part, weight, (1, 0))
        gradient = gradient + dot(grad_part[:, columns], weight, (1, 1))
        if step < planes - 1:
            gradient = lax.optimization_barrier(gradient)
        sums.append(jnp.sum(cotangent_part[:, columns].astype(f32) * out, axis=0))
        partial.append(out.astype(bf16))

    early = jnp.concatenate(partial[:-1], axis=1)
    late = partial[-1]
    (early_slots,) = exchange(
        [rows_to_slots(rows)], [early],
        [jax.ShapeDtypeStruct((CHIPS, rows, early.shape[1]), bf16)], 3,
    )
    sums = jnp.broadcast_to(jnp.concatenate(sums)[None], (8, outputs))
    sums = reorder(from_arrival, [sums], f32, False, info, planes)[0]
    sums = (sums + jnp.sum(cot_own * adapter, axis=0)) / norm
    late_slots, input_gradient, grad_magnitude = exchange(
        [rows_to_slots(rows), columns_to_rows(rows, depth)], [late, gradient.astype(bf16)],
        [jax.ShapeDtypeStruct((CHIPS, rows, block), bf16),
         jax.ShapeDtypeStruct((rows, features), bf16)], 4,
        "sum", sums.reshape(outputs // 128, 128),
    )
    grad_magnitude = grad_magnitude.reshape(outputs)
    base = jnp.concatenate(
        [jnp.sum(early_slots.astype(f32), axis=0), jnp.sum(late_slots.astype(f32), axis=0)], axis=1
    )
    output = reorder(finish_block, [base, adapter, scale[None]], bf16, False, info, planes,
                     [pltpu.VMEM((rows, block // 2), f32)])
    return (output, input_gradient, grad_down * factor, grad_up * factor, grad_magnitude * factor)


def on_device(tokens, frozen_matrix, adapter_down_factor, adapter_up_factor, magnitude, cotangent):
    tok_rows = tokens.shape[0]
    local_portion = adapter_up_factor.shape[1]
    gathered_up_factor, full_magnitude = (
        lax.all_gather(adapter_up_factor, "tensor", axis=1, tiled=True),
        lax.all_gather(magnitude, "tensor", axis=0, tiled=True),
    )
    rank_partial = jnp.dot(tokens, adapter_down_factor, preferred_element_type=jnp.float32)
    rank_activation = lax.psum(rank_partial, "tensor").astype(jnp.bfloat16)
    piece = lax.all_gather(frozen_matrix, "dp", axis=1, tiled=True)
    result = jnp.dot(tokens, piece, preferred_element_type=jnp.float32)
    combined_output = piece.astype(jnp.float32) + jnp.dot(
        adapter_down_factor, gathered_up_factor, preferred_element_type=jnp.float32
    )
    squares = jnp.sum(combined_output * combined_output, axis=0)
    square_part = squares
    squares = lax.psum(square_part, "tensor")
    norm = jnp.sqrt(squares + epsilon)
    scale = full_magnitude.astype(jnp.float32) / norm
    frozen_output = lax.psum_scatter(result, "tensor", scatter_dimension=1, tiled=True)
    shard_start = lax.axis_index("tensor") * local_portion
    merged_weight = frozen_output + jnp.dot(
        rank_activation, adapter_up_factor, preferred_element_type=jnp.float32
    )
    own_scale = lax.dynamic_slice_in_dim(scale, shard_start, local_portion, 0)
    own_norm_vals = lax.dynamic_slice_in_dim(norm, shard_start, local_portion, 0)
    output = (merged_weight * own_scale).astype(jnp.bfloat16)
    rescaled_gradient = (cotangent.astype(jnp.float32) * scale).astype(jnp.bfloat16)
    rank_gradient = jnp.dot(
        rescaled_gradient, gathered_up_factor.T, preferred_element_type=jnp.float32
    ).astype(jnp.bfloat16)
    gradient_running_total = lax.dot_general(
        rescaled_gradient,
        lax.all_gather(frozen_matrix, "dp", axis=1, tiled=True),
        (((1,), (1,)), ((), ())),
        preferred_element_type=jnp.float32,
    )
    input_gradient = (
        gradient_running_total
        + jnp.dot(rank_gradient, adapter_down_factor.T, preferred_element_type=jnp.float32)
    ).astype(jnp.bfloat16)
    own_grad = lax.dynamic_slice_in_dim(rescaled_gradient, shard_start, local_portion, 1)
    own_cotangent = lax.dynamic_slice_in_dim(cotangent, shard_start, local_portion, 1).astype(
        jnp.float32
    )
    down_part = lax.dot_general(
        tokens, rank_gradient, (((0,), (0,)), ((), ())), preferred_element_type=jnp.float32
    )
    up_part = lax.dot_general(
        rank_activation, own_grad, (((0,), (0,)), ((), ())), preferred_element_type=jnp.float32
    )
    magnitude_part = jnp.sum(own_cotangent * merged_weight / own_norm_vals, axis=0)
    grad_down, grad_up, grad_magnitude = lax.psum((down_part, up_part, magnitude_part), "dp")
    factor = 1.0 / math.sqrt(tok_rows * lax.axis_size("dp"))
    return (output, input_gradient, grad_down * factor, grad_up * factor, grad_magnitude * factor)


def solution(mesh):
    planes = mesh.shape["dp"] // PLANE
    in_planes = mesh.shape["tensor"] == 1 and mesh.shape["dp"] == PLANE * planes and planes > 1
    return jax.shard_map(
        on_plane if in_planes else on_device,
        mesh=mesh,
        in_specs=(
            P("dp", "tensor"),
            P("tensor", "dp"),
            P("tensor", None),
            P(None, "tensor"),
            P("tensor"),
            P("dp", None),
        ),
        out_specs=(
            P("dp", "tensor"),
            P("dp", "tensor"),
            P("tensor", None),
            P(None, "tensor"),
            P("tensor"),
        ),
        check_vma=False,
    )
```

```python
import functools
import math

import jax
import jax.numpy as jnp
from jax import lax
from jax.experimental import pallas as pl
from jax.experimental.pallas import tpu as pltpu
from jax.sharding import PartitionSpec as P

epsilon = 1e-06

CHIPS = 4
CORES = 2
PLANE = CHIPS * CORES


def place():
    me = lax.axis_index("dp")
    return me // PLANE, (me % PLANE) // CORES, me % CORES


def exchange_kernel(views, vector, *refs):
    count = len(views)
    ends = count + (vector is not None)
    if vector == "sum":
        ends += 1
    sources, targets = refs[:count], refs[ends : ends + count]
    small_in, small_out = refs[count], refs[ends + count]
    terms, totals = refs[ends - 1], refs[2 * ends - 1]
    scratch = refs[2 * ends :]
    send_sem, recv_sem, local_sem = scratch[:3]
    me = lax.axis_index("dp")
    planes = lax.axis_size("dp") // PLANE
    plane, chip, core = place()
    spot = me % PLANE
    base = me - chip * CORES
    sibling = me - core + (core + 1) % CORES

    def remote(source, target, send, recv, device):
        return pltpu.make_async_remote_copy(
            src_ref=source, dst_ref=target, send_sem=send, recv_sem=recv,
            device_id={"dp": device}, device_id_type=pl.DeviceIdType.MESH,
        )

    if vector is None:
        partners = [base + ((chip + hop) % CHIPS) * CORES for hop in range(1, CHIPS)]
    else:
        above = [(plane + hop) % planes * PLANE + spot for hop in range(1, planes)]
        beside = [plane * PLANE + (spot + hop) % PLANE for hop in range(1, PLANE)]
        partners = above + beside
        group = {}
        for turn in range(CORES):
            for hop in range(planes):
                if turn + hop > 0:
                    group[turn, hop] = (
                        (plane + hop) % planes * PLANE + chip * CORES + (core + turn) % CORES
                    )
        if vector == "sum":
            partners = partners + [group[1, hop] for hop in range(1, planes)]
    barrier = pltpu.get_barrier_semaphore()
    for device in partners:
        pl.semaphore_signal(
            barrier, inc=1, device_id={"dp": device}, device_id_type=pl.DeviceIdType.MESH
        )
    pl.semaphore_wait(barrier, len(partners))

    line = []
    if vector is not None:
        line_send, line_recv, flat_send, flat_recv = scratch[3:7]
        if vector == "gather":
            own = small_out.at[spot, plane]
            keep = pltpu.make_async_copy(small_in, own, local_sem.at[count])
            keep.start()
            start = small_in
        else:
            line_sum, flat_sum, parts, total, part_send, part_recv, total_send, total_recv = scratch[7:]
            mine = parts.at[core, plane]
            keep = pltpu.make_async_copy(terms.at[core, plane], mine, local_sem.at[count])
            keep.start()
            shares = []
            for (turn, hop), device in group.items():
                theirs = terms.at[(core + turn) % CORES, (plane + hop) % planes]
                shares.append(remote(theirs, mine, part_send.at[turn, hop],
                                     part_recv.at[turn, hop], device))
                shares[-1].start()
            own = line_sum.at[plane]
            own[...] = small_in[...]
            start = own
        for hop, device in enumerate(above):
            line.append(remote(start, own, line_send.at[hop], line_recv.at[hop], device))
            line[-1].start()
    copies = []
    for number, view in enumerate(views):
        for hop in (2, 1, 3):
            other = (chip + hop) % CHIPS
            source, target = view(sources[number], targets[number], other, chip)
            copies.append(remote(source, target, send_sem.at[number, hop],
                                 recv_sem.at[number, hop], base + other * CORES))
            copies[-1].start()
    for number, view in enumerate(views):
        source, target = view(sources[number], targets[number], chip, chip)
        copies.append(pltpu.make_async_copy(source, target, local_sem.at[number]))
        copies[-1].start()
    if vector is not None:
        for copy in line:
            copy.wait()
        if vector == "gather":
            keep.wait()
            block = small_out.at[spot]
        else:
            block = flat_sum.at[spot]
            block[...] = functools.reduce(lambda x, y: x + y, [line_sum[i] for i in range(planes)])
        for hop, device in enumerate(beside):
            copies.append(remote(block, block, flat_send.at[hop], flat_recv.at[hop], device))
            copies[-1].start()
    if vector == "sum":
        for copy in shares:
            copy.wait()
        keep.wait()
        total[...] = functools.reduce(
            lambda x, y: x + y, [parts[k, z] for k in range(CORES) for z in range(planes)]
        )
        place_of = totals.at[core, chip, plane]
        keep = pltpu.make_async_copy(total, place_of, local_sem.at[count])
        keep.start()
        stage = [remote(total, place_of, total_send.at[0, hop], total_recv.at[0, hop], device)
                 for hop, device in enumerate(above)]
        for copy in stage:
            copy.start()
        for copy in stage:
            copy.wait()
        keep.wait()
        column = totals.at[core, chip]
        stage = [remote(column, column, total_send.at[1, hop], total_recv.at[1, hop],
                        base + ((chip + hop) % CHIPS) * CORES) for hop in range(1, CHIPS)]
        for copy in stage:
            copy.start()
        for copy in stage:
            copy.wait()
        side = totals.at[core]
        copies.append(remote(side, side, total_send.at[2, 0], total_recv.at[2, 0], sibling))
        copies[-1].start()
    for copy in copies:
        copy.wait()
    if vector == "sum":
        small_out[...] = functools.reduce(lambda x, y: x + y, [flat_sum[i] for i in range(PLANE)])


def exchange(views, sources, shapes, collective_id, vector=None, small=None, terms=None):
    count = len(views)
    planes = lax.axis_size("dp") // PLANE
    moved = sum(math.prod(s.shape) * s.dtype.itemsize for s in shapes)
    sources, shapes = list(sources), list(shapes)
    specs = [pl.BlockSpec(memory_space=pl.ANY)] * count
    dma = pltpu.SemaphoreType.DMA
    scratch = [dma((count, CHIPS)), dma((count, CHIPS)), dma((count + 1,))]
    if vector is not None:
        sources.append(small)
        scratch += [dma((planes,)), dma((planes,)), dma((PLANE,)), dma((PLANE,))]
        if vector == "gather":
            specs = specs + [pl.BlockSpec(memory_space=pl.ANY)]
            shapes.append(jax.ShapeDtypeStruct((PLANE, planes) + small.shape, small.dtype))
        else:
            specs = specs + [pl.BlockSpec(memory_space=pltpu.VMEM)]
            shapes.append(jax.ShapeDtypeStruct(small.shape, small.dtype))
            scratch += [pltpu.VMEM((planes,) + small.shape, small.dtype),
                        pltpu.VMEM((PLANE,) + small.shape, small.dtype)]
            sources.append(terms)
            specs = specs + [pl.BlockSpec(memory_space=pl.ANY)]
            piece = terms.shape[2:]
            shapes.append(jax.ShapeDtypeStruct((CORES, CHIPS, planes) + piece, terms.dtype))
            scratch += [pltpu.VMEM(terms.shape, terms.dtype), pltpu.VMEM(piece, terms.dtype),
                        dma((CORES, planes)), dma((CORES, planes)), dma((3, 4)), dma((3, 4))]
    return pl.pallas_call(
        functools.partial(exchange_kernel, views, vector),
        out_shape=shapes,
        in_specs=specs,
        out_specs=specs,
        scratch_shapes=scratch,
        compiler_params=pltpu.CompilerParams(
            collective_id=collective_id, has_side_effects=True
        ),
        cost_estimate=pl.CostEstimate(flops=0, bytes_accessed=40 * moved, transcendentals=0),
    )(*sources)


def ring_kernel(views, steps, *refs):
    count = len(views)
    blocks, sources = refs[0], refs[1 : 1 + count]
    weights, refs = refs[1 + count : 2 + count + steps], refs[2 + count + steps :]
    targets = refs[:count]
    send_sem, recv_sem, ring_send, ring_recv, side_send, side_recv, local_sem = refs[count:]
    me = lax.axis_index("dp")
    size = lax.axis_size("dp")
    plane, chip, core = place()
    base = me - chip * CORES
    sibling = me - core + (core + 1) % CORES
    after, before = (me + PLANE) % size, (me + size - PLANE) % size
    width = blocks.shape[2]

    def remote(source, target, send, recv, device):
        return pltpu.make_async_remote_copy(
            src_ref=source, dst_ref=target, send_sem=send, recv_sem=recv,
            device_id={"dp": device}, device_id_type=pl.DeviceIdType.MESH,
        )

    partners = [base + ((chip + hop) % CHIPS) * CORES for hop in range(1, CHIPS)]
    partners += [sibling, after, before]
    barrier = pltpu.get_barrier_semaphore()
    for device in partners:
        pl.semaphore_signal(
            barrier, inc=1, device_id={"dp": device}, device_id_type=pl.DeviceIdType.MESH
        )
    pl.semaphore_wait(barrier, len(partners))

    def spot(step, side, other):
        return weights[step].at[:, pl.ds((side * 2 + other) * width, width)]

    def send(step):
        ring, across = [], []
        for side, device in enumerate((after, before)):
            source = blocks.at[side] if step == 0 else spot(step, side, 0)
            if step < steps:
                ring.append(remote(source, spot(step + 1, side, 0), ring_send.at[step, side],
                                   ring_recv.at[step, side], device))
                ring[-1].start()
            across.append(remote(source, spot(step, side, 1), side_send.at[step, side],
                                 side_recv.at[step, side], sibling))
            across[-1].start()
        return ring, across

    ring, copies = send(0)
    for number, view in enumerate(views):
        for hop in (2, 1, 3):
            other = (chip + hop) % CHIPS
            source, target = view(sources[number], targets[number], other, chip)
            copies.append(remote(source, target, send_sem.at[number, hop],
                                 recv_sem.at[number, hop], base + other * CORES))
            copies[-1].start()
    for number, view in enumerate(views):
        source, target = view(sources[number], targets[number], chip, chip)
        copies.append(pltpu.make_async_copy(source, target, local_sem.at[number]))
        copies[-1].start()
    for side in range(2):
        copies.append(pltpu.make_async_copy(
            blocks.at[side], spot(0, side, 0), local_sem.at[count + side]))
        copies[-1].start()
    for step in range(1, steps + 1):
        for copy in ring:
            copy.wait()
        ring, across = send(step)
        copies += across
    for copy in copies:
        copy.wait()


def ring_exchange(blocks, steps, views, sources, shapes, collective_id):
    count = len(views)
    _, depth, width = blocks.shape
    dma = pltpu.SemaphoreType.DMA
    anywhere = pl.BlockSpec(memory_space=pl.ANY)
    return pl.pallas_call(
        functools.partial(ring_kernel, views, steps),
        out_shape=[jax.ShapeDtypeStruct((depth, 4 * width), blocks.dtype)] * (steps + 1) + list(shapes),
        in_specs=[anywhere] * (count + 1),
        out_specs=[anywhere] * (count + steps + 1),
        scratch_shapes=[dma((count, CHIPS)), dma((count, CHIPS)),
                        dma((steps + 1, 2)), dma((steps + 1, 2)),
                        dma((steps + 1, 2)), dma((steps + 1, 2)), dma((count + 2,))],
        compiler_params=pltpu.CompilerParams(
            collective_id=collective_id, has_side_effects=True
        ),
        cost_estimate=pl.CostEstimate(flops=0, bytes_accessed=400_000_000, transcendentals=0),
    )(blocks, *sources)


def to_arrival(info, x_ref, y_ref):
    width = x_ref.shape[1] // 4
    core = info[1]
    x = [x_ref[:, i * width : (i + 1) * width] for i in range(4)]
    for i, (zero, one) in enumerate(((0, 1), (2, 3), (1, 0), (3, 2))):
        y_ref[:, i * width : (i + 1) * width] = jnp.where(core == 0, x[zero], x[one])


def from_arrival(info, x_ref, y_ref):
    width = x_ref.shape[1] // 4
    core = info[1]
    x = [x_ref[:, i * width : (i + 1) * width] for i in range(4)]
    for i, (zero, one) in enumerate(((0, 2), (2, 0), (1, 3), (3, 1))):
        y_ref[:, i * width : (i + 1) * width] = jnp.where(core == 0, x[zero], x[one])


def finish_block(info, x_ref, adapter_ref, scale_ref, y_ref, base_ref):
    from_arrival(info, x_ref, base_ref)
    y_ref[...] = ((base_ref[...] + adapter_ref[...]) * scale_ref[...]).astype(y_ref.dtype)


def reorder(kernel, arrays, kind, forward, info, planes, scratch=()):
    rows, outputs = arrays[0].shape
    block = outputs // planes // 2

    def there(i, info):
        number, side, plane = i // 2, i % 2, info[0]
        falling = (plane + planes - number) % planes
        rising = (plane + number) % planes if forward else (number + planes - plane) % planes
        return 0, jnp.where(side == 0, falling, rising) * 2 + side

    def here(i, info):
        return 0, i

    specs = [pl.BlockSpec((rows, block), there)]
    specs += [pl.BlockSpec((a.shape[0], block), here) for a in arrays[1:]]
    return pl.pallas_call(
        kernel,
        out_shape=jax.ShapeDtypeStruct((rows, outputs), kind),
        grid_spec=pltpu.PrefetchScalarGridSpec(
            num_scalar_prefetch=1,
            grid=(planes * 2,),
            in_specs=specs,
            out_specs=pl.BlockSpec((rows, block), here),
            scratch_shapes=list(scratch),
        ),
    )(info, *arrays)


def rows_to_columns(depth):
    def view(source, target, other, chip):
        rows = source.shape[0]
        return (
            source.at[:, pl.ds(pl.multiple_of(other * depth, 128), depth)],
            target.at[pl.ds(pl.multiple_of(chip * rows, 128), rows), :],
        )
    return view


def columns_to_rows(rows, depth):
    def view(source, target, other, chip):
        return (
            source.at[pl.ds(pl.multiple_of(other * rows, 128), rows), :],
            target.at[:, pl.ds(pl.multiple_of(chip * depth, 128), depth)],
        )
    return view


def whole_rows(source, target, other, chip):
    rows = source.shape[0]
    return source, target.at[pl.ds(pl.multiple_of(chip * rows, 128), rows), :]


def rows_to_slots(rows):
    def view(source, target, other, chip):
        return source.at[pl.ds(pl.multiple_of(other * rows, 128), rows), :], target.at[chip]
    return view


def frozen_view(depth, width):
    def view(source, target, other, chip):
        return (
            source.at[pl.ds(pl.multiple_of(other * depth, 128), depth), :],
            target.at[chip // 2, :, pl.ds(pl.multiple_of((chip % 2) * width, 128), width)],
        )
    return view


def dot(a, b, contract):
    return lax.dot_general(a, b, ((contract[:1], contract[1:]), ((), ())),
                           preferred_element_type=jnp.float32)


def on_plane(tokens, frozen, down, up, magnitude, cotangent):
    rows, features = tokens.shape
    width = frozen.shape[1]
    outputs = cotangent.shape[1]
    size = lax.axis_size("dp")
    planes = size // PLANE
    depth = features // CHIPS
    block = outputs // planes
    me = lax.axis_index("dp")
    plane, chip, core = place()
    info = jnp.stack([plane, core]).astype(jnp.int32)
    f32, bf16 = jnp.float32, jnp.bfloat16

    own_up = lax.dynamic_slice_in_dim(up, me * width, width, 1)
    combined = frozen.astype(f32) + jnp.dot(down, own_up, preferred_element_type=f32)
    squares = jnp.broadcast_to(jnp.sum(combined * combined, axis=0)[None], (8, width))
    blocks, squares = exchange(
        [frozen_view(depth, width)], [frozen],
        [jax.ShapeDtypeStruct((2, depth, 2 * width), bf16)], 1, "gather", squares,
    )
    rank_act = jnp.dot(tokens, down, preferred_element_type=f32).astype(bf16)
    steps = planes - 2
    *weights, tokens_part, cotangent_part, rank_part = ring_exchange(
        blocks, steps, [rows_to_columns(depth), whole_rows, whole_rows],
        [tokens, reorder(to_arrival, [cotangent], bf16, True, info, planes),
         jnp.pad(rank_act, ((0, 0), (0, 128 - rank_act.shape[1] % 128)))],
        [jax.ShapeDtypeStruct((CHIPS * rows, depth), bf16),
         jax.ShapeDtypeStruct((CHIPS * rows, outputs), bf16),
         jax.ShapeDtypeStruct((CHIPS * rows, 128), bf16)], 2,
    )

    forward = [(i, (i + PLANE) % size) for i in range(size)]
    backward = [((i + PLANE) % size, i) for i in range(size)]
    across = [(i, i - i % CORES + (i + 1) % CORES) for i in range(size)]
    falling = lax.ppermute(weights[steps][:, : 2 * width], "dp", forward)
    rising = lax.ppermute(weights[steps][:, 4 * width : 6 * width], "dp", backward)
    last = jnp.concatenate(
        [falling, lax.ppermute(falling, "dp", across), rising, lax.ppermute(rising, "dp", across)],
        axis=1,
    )

    norm = jnp.sqrt(squares[:, :, 0, :].transpose(1, 0, 2).reshape(outputs) + epsilon)
    scale = magnitude.astype(f32) / norm
    scale_rows = jnp.broadcast_to(scale[None], (8, outputs))
    scale_arrival = reorder(to_arrival, [scale_rows], f32, True, info, planes)[:1]

    adapter = jnp.dot(rank_act, up, preferred_element_type=f32)
    cot_own = cotangent.astype(f32)
    factor = 1.0 / math.sqrt(rows * size)

    grad_part = (cotangent_part.astype(f32) * scale_arrival).astype(bf16)
    up_arrival = reorder(to_arrival, [up], bf16, True, info, planes)
    back_part = dot(grad_part, up_arrival, (1, 1)).astype(bf16)
    down_rows = lax.dynamic_slice_in_dim(down, chip * depth, depth, 0)
    gradient = dot(back_part, down_rows, (1, 1))

    rank = up.shape[0]
    down_part = dot(back_part, tokens_part, (0, 0))
    up_part = dot(rank_part, grad_part, (0, 0))[:rank]
    up_part = reorder(from_arrival, [up_part], f32, False, info, planes)
    up_part = lax.dynamic_slice_in_dim(up_part, chip * (outputs // CHIPS), outputs // CHIPS, 1)
    terms = jnp.concatenate([down_part, up_part], axis=1)
    terms = terms.reshape(CORES, planes, rank // (CORES * planes), terms.shape[1])

    partial, sums = [], []
    for step in range(planes):
        weight = weights[step] if step <= steps else last
        columns = slice(step * block, (step + 1) * block)
        out = dot(tokens_part, weight, (1, 0))
        gradient = gradient + dot(grad_part[:, columns], weight, (1, 1))
        if step < planes - 1:
            gradient = lax.optimization_barrier(gradient)
        sums.append(jnp.sum(cotangent_part[:, columns].astype(f32) * out, axis=0))
        partial.append(out.astype(bf16))

    early = jnp.concatenate(partial[:-1], axis=1)
    late = partial[-1]
    (early_slots,) = exchange(
        [rows_to_slots(rows)], [early],
        [jax.ShapeDtypeStruct((CHIPS, rows, early.shape[1]), bf16)], 3,
    )
    sums = jnp.broadcast_to(jnp.concatenate(sums)[None], (8, outputs))
    sums = reorder(from_arrival, [sums], f32, False, info, planes)[0]
    sums = (sums + jnp.sum(cot_own * adapter, axis=0)) / norm
    early_slots, late, sums = lax.optimization_barrier((early_slots, late, sums))
    late_slots, input_gradient, grad_magnitude, totals = exchange(
        [rows_to_slots(rows), columns_to_rows(rows, depth)], [late, gradient.astype(bf16)],
        [jax.ShapeDtypeStruct((CHIPS, rows, block), bf16),
         jax.ShapeDtypeStruct((rows, features), bf16)], 4,
        "sum", sums.reshape(outputs // 128, 128), terms,
    )
    totals = totals.transpose(0, 2, 3, 1, 4) * factor
    grad_down = totals[..., :depth].reshape(rank, features).T
    grad_up = totals[..., depth:].reshape(rank, outputs)
    grad_magnitude = grad_magnitude.reshape(outputs)
    base = jnp.concatenate(
        [jnp.sum(early_slots.astype(f32), axis=0), jnp.sum(late_slots.astype(f32), axis=0)], axis=1
    )
    output = reorder(finish_block, [base, adapter, scale[None]], bf16, False, info, planes,
                     [pltpu.VMEM((rows, block // 2), f32)])
    return (output, input_gradient, grad_down, grad_up, grad_magnitude * factor)


def on_device(tokens, frozen_matrix, adapter_down_factor, adapter_up_factor, magnitude, cotangent):
    tok_rows = tokens.shape[0]
    local_portion = adapter_up_factor.shape[1]
    gathered_up_factor, full_magnitude = (
        lax.all_gather(adapter_up_factor, "tensor", axis=1, tiled=True),
        lax.all_gather(magnitude, "tensor", axis=0, tiled=True),
    )
    rank_partial = jnp.dot(tokens, adapter_down_factor, preferred_element_type=jnp.float32)
    rank_activation = lax.psum(rank_partial, "tensor").astype(jnp.bfloat16)
    piece = lax.all_gather(frozen_matrix, "dp", axis=1, tiled=True)
    result = jnp.dot(tokens, piece, preferred_element_type=jnp.float32)
    combined_output = piece.astype(jnp.float32) + jnp.dot(
        adapter_down_factor, gathered_up_factor, preferred_element_type=jnp.float32
    )
    squares = jnp.sum(combined_output * combined_output, axis=0)
    square_part = squares
    squares = lax.psum(square_part, "tensor")
    norm = jnp.sqrt(squares + epsilon)
    scale = full_magnitude.astype(jnp.float32) / norm
    frozen_output = lax.psum_scatter(result, "tensor", scatter_dimension=1, tiled=True)
    shard_start = lax.axis_index("tensor") * local_portion
    merged_weight = frozen_output + jnp.dot(
        rank_activation, adapter_up_factor, preferred_element_type=jnp.float32
    )
    own_scale = lax.dynamic_slice_in_dim(scale, shard_start, local_portion, 0)
    own_norm_vals = lax.dynamic_slice_in_dim(norm, shard_start, local_portion, 0)
    output = (merged_weight * own_scale).astype(jnp.bfloat16)
    rescaled_gradient = (cotangent.astype(jnp.float32) * scale).astype(jnp.bfloat16)
    rank_gradient = jnp.dot(
        rescaled_gradient, gathered_up_factor.T, preferred_element_type=jnp.float32
    ).astype(jnp.bfloat16)
    gradient_running_total = lax.dot_general(
        rescaled_gradient,
        lax.all_gather(frozen_matrix, "dp", axis=1, tiled=True),
        (((1,), (1,)), ((), ())),
        preferred_element_type=jnp.float32,
    )
    input_gradient = (
        gradient_running_total
        + jnp.dot(rank_gradient, adapter_down_factor.T, preferred_element_type=jnp.float32)
    ).astype(jnp.bfloat16)
    own_grad = lax.dynamic_slice_in_dim(rescaled_gradient, shard_start, local_portion, 1)
    own_cotangent = lax.dynamic_slice_in_dim(cotangent, shard_start, local_portion, 1).astype(
        jnp.float32
    )
    down_part = lax.dot_general(
        tokens, rank_gradient, (((0,), (0,)), ((), ())), preferred_element_type=jnp.float32
    )
    up_part = lax.dot_general(
        rank_activation, own_grad, (((0,), (0,)), ((), ())), preferred_element_type=jnp.float32
    )
    magnitude_part = jnp.sum(own_cotangent * merged_weight / own_norm_vals, axis=0)
    grad_down, grad_up, grad_magnitude = lax.psum((down_part, up_part, magnitude_part), "dp")
    factor = 1.0 / math.sqrt(tok_rows * lax.axis_size("dp"))
    return (output, input_gradient, grad_down * factor, grad_up * factor, grad_magnitude * factor)


def solution(mesh):
    planes = mesh.shape["dp"] // PLANE
    in_planes = mesh.shape["tensor"] == 1 and mesh.shape["dp"] == PLANE * planes and planes == 4
    return jax.shard_map(
        on_plane if in_planes else on_device,
        mesh=mesh,
        in_specs=(
            P("dp", "tensor"),
            P("tensor", "dp"),
            P("tensor", None),
            P(None, "tensor"),
            P("tensor"),
            P("dp", None),
        ),
        out_specs=(
            P("dp", "tensor"),
            P("dp", "tensor"),
            P("tensor", None),
            P(None, "tensor"),
            P("tensor"),
        ),
        check_vma=False,
    )
```

```python
import functools
import math

import jax
import jax.numpy as jnp
from jax import lax
from jax.experimental import pallas as pl
from jax.experimental.pallas import tpu as pltpu
from jax.sharding import PartitionSpec as P

epsilon = 1e-06

CHIPS = 4
CORES = 2
PLANE = CHIPS * CORES


def place():
    me = lax.axis_index("dp")
    return me // PLANE, (me % PLANE) // CORES, me % CORES


def exchange_kernel(views, vector, *refs):
    count = len(views)
    ends = count + (vector is not None)
    if vector == "sum":
        ends += 1
    sources, targets = refs[:count], refs[ends : ends + count]
    small_in, small_out = refs[count], refs[ends + count]
    terms, totals = refs[ends - 1], refs[2 * ends - 1]
    scratch = refs[2 * ends :]
    send_sem, recv_sem, local_sem = scratch[:3]
    me = lax.axis_index("dp")
    planes = lax.axis_size("dp") // PLANE
    plane, chip, core = place()
    spot = me % PLANE
    base = me - chip * CORES
    sibling = me - core + (core + 1) % CORES

    def remote(source, target, send, recv, device):
        return pltpu.make_async_remote_copy(
            src_ref=source, dst_ref=target, send_sem=send, recv_sem=recv,
            device_id={"dp": device}, device_id_type=pl.DeviceIdType.MESH,
        )

    if vector is None:
        partners = [base + ((chip + hop) % CHIPS) * CORES for hop in range(1, CHIPS)]
    else:
        above = [(plane + hop) % planes * PLANE + spot for hop in range(1, planes)]
        beside = [plane * PLANE + (spot + hop) % PLANE for hop in range(1, PLANE)]
        partners = above + beside
        group = {}
        for turn in range(CORES):
            for hop in range(planes):
                if turn + hop > 0:
                    group[turn, hop] = (
                        (plane + hop) % planes * PLANE + chip * CORES + (core + turn) % CORES
                    )
        if vector == "sum":
            partners = partners + [group[1, hop] for hop in range(1, planes)]
    barrier = pltpu.get_barrier_semaphore()
    for device in partners:
        pl.semaphore_signal(
            barrier, inc=1, device_id={"dp": device}, device_id_type=pl.DeviceIdType.MESH
        )
    pl.semaphore_wait(barrier, len(partners))

    line = []
    if vector is not None:
        line_send, line_recv, flat_send, flat_recv = scratch[3:7]
        if vector == "gather":
            own = small_out.at[spot, plane]
            keep = pltpu.make_async_copy(small_in, own, local_sem.at[count])
            keep.start()
            start = small_in
        else:
            line_sum, flat_sum, parts, total, part_send, part_recv, total_send, total_recv = scratch[7:]
            mine = parts.at[core, plane]
            keep = pltpu.make_async_copy(terms.at[core, plane], mine, local_sem.at[count])
            keep.start()
            shares = []
            for (turn, hop), device in group.items():
                theirs = terms.at[(core + turn) % CORES, (plane + hop) % planes]
                shares.append(remote(theirs, mine, part_send.at[turn, hop],
                                     part_recv.at[turn, hop], device))
                shares[-1].start()
            own = line_sum.at[plane]
            own[...] = small_in[...]
            start = own
        for hop, device in enumerate(above):
            line.append(remote(start, own, line_send.at[hop], line_recv.at[hop], device))
            line[-1].start()
    copies = []
    for number, view in enumerate(views):
        for hop in (2, 1, 3):
            other = (chip + hop) % CHIPS
            source, target = view(sources[number], targets[number], other, chip)
            copies.append(remote(source, target, send_sem.at[number, hop],
                                 recv_sem.at[number, hop], base + other * CORES))
            copies[-1].start()
    for number, view in enumerate(views):
        source, target = view(sources[number], targets[number], chip, chip)
        copies.append(pltpu.make_async_copy(source, target, local_sem.at[number]))
        copies[-1].start()
    if vector is not None:
        for copy in line:
            copy.wait()
        if vector == "gather":
            keep.wait()
            block = small_out.at[spot]
        else:
            block = flat_sum.at[spot]
            block[...] = functools.reduce(lambda x, y: x + y, [line_sum[i] for i in range(planes)])
        for hop, device in enumerate(beside):
            copies.append(remote(block, block, flat_send.at[hop], flat_recv.at[hop], device))
            copies[-1].start()
    if vector == "sum":
        for copy in shares:
            copy.wait()
        keep.wait()
        total[...] = functools.reduce(
            lambda x, y: x + y, [parts[k, z] for k in range(CORES) for z in range(planes)]
        )
        place_of = totals.at[core, chip, plane]
        keep = pltpu.make_async_copy(total, place_of, local_sem.at[count])
        keep.start()
        stage = [remote(total, place_of, total_send.at[0, hop], total_recv.at[0, hop], device)
                 for hop, device in enumerate(above)]
        for copy in stage:
            copy.start()
        for copy in stage:
            copy.wait()
        keep.wait()
        column = totals.at[core, chip]
        stage = [remote(column, column, total_send.at[1, hop], total_recv.at[1, hop],
                        base + ((chip + hop) % CHIPS) * CORES) for hop in range(1, CHIPS)]
        for copy in stage:
            copy.start()
        for copy in stage:
            copy.wait()
        side = totals.at[core]
        copies.append(remote(side, side, total_send.at[2, 0], total_recv.at[2, 0], sibling))
        copies[-1].start()
    for copy in copies:
        copy.wait()
    if vector == "sum":
        small_out[...] = functools.reduce(lambda x, y: x + y, [flat_sum[i] for i in range(PLANE)])


def exchange(views, sources, shapes, collective_id, vector=None, small=None, terms=None):
    count = len(views)
    planes = lax.axis_size("dp") // PLANE
    moved = sum(math.prod(s.shape) * s.dtype.itemsize for s in shapes)
    sources, shapes = list(sources), list(shapes)
    specs = [pl.BlockSpec(memory_space=pl.ANY)] * count
    dma = pltpu.SemaphoreType.DMA
    scratch = [dma((count, CHIPS)), dma((count, CHIPS)), dma((count + 1,))]
    if vector is not None:
        sources.append(small)
        scratch += [dma((planes,)), dma((planes,)), dma((PLANE,)), dma((PLANE,))]
        if vector == "gather":
            specs = specs + [pl.BlockSpec(memory_space=pl.ANY)]
            shapes.append(jax.ShapeDtypeStruct((PLANE, planes) + small.shape, small.dtype))
        else:
            specs = specs + [pl.BlockSpec(memory_space=pltpu.VMEM)]
            shapes.append(jax.ShapeDtypeStruct(small.shape, small.dtype))
            scratch += [pltpu.VMEM((planes,) + small.shape, small.dtype),
                        pltpu.VMEM((PLANE,) + small.shape, small.dtype)]
            sources.append(terms)
            specs = specs + [pl.BlockSpec(memory_space=pl.ANY)]
            piece = terms.shape[2:]
            shapes.append(jax.ShapeDtypeStruct((CORES, CHIPS, planes) + piece, terms.dtype))
            scratch += [pltpu.VMEM(terms.shape, terms.dtype), pltpu.VMEM(piece, terms.dtype),
                        dma((CORES, planes)), dma((CORES, planes)), dma((3, 4)), dma((3, 4))]
    return pl.pallas_call(
        functools.partial(exchange_kernel, views, vector),
        out_shape=shapes,
        in_specs=specs,
        out_specs=specs,
        scratch_shapes=scratch,
        compiler_params=pltpu.CompilerParams(
            collective_id=collective_id, has_side_effects=True
        ),
        cost_estimate=pl.CostEstimate(flops=0, bytes_accessed=40 * moved, transcendentals=0),
    )(*sources)


def ring_kernel(views, steps, *refs):
    count = len(views)
    blocks, sources = refs[0], refs[1 : 1 + count]
    weights, refs = refs[1 + count : 2 + count + steps], refs[2 + count + steps :]
    targets = refs[:count]
    send_sem, recv_sem, ring_send, ring_recv, side_send, side_recv, local_sem = refs[count:]
    me = lax.axis_index("dp")
    size = lax.axis_size("dp")
    plane, chip, core = place()
    base = me - chip * CORES
    sibling = me - core + (core + 1) % CORES
    after, before = (me + PLANE) % size, (me + size - PLANE) % size
    width = blocks.shape[2]

    def remote(source, target, send, recv, device):
        return pltpu.make_async_remote_copy(
            src_ref=source, dst_ref=target, send_sem=send, recv_sem=recv,
            device_id={"dp": device}, device_id_type=pl.DeviceIdType.MESH,
        )

    partners = [base + ((chip + hop) % CHIPS) * CORES for hop in range(1, CHIPS)]
    partners += [sibling, after, before]
    barrier = pltpu.get_barrier_semaphore()
    for device in partners:
        pl.semaphore_signal(
            barrier, inc=1, device_id={"dp": device}, device_id_type=pl.DeviceIdType.MESH
        )
    pl.semaphore_wait(barrier, len(partners))

    def spot(step, side, other):
        return weights[step].at[:, pl.ds((side * 2 + other) * width, width)]

    def send(step):
        ring, across = [], []
        for side, device in enumerate((after, before)):
            source = blocks.at[side] if step == 0 else spot(step, side, 0)
            if step < steps:
                ring.append(remote(source, spot(step + 1, side, 0), ring_send.at[step, side],
                                   ring_recv.at[step, side], device))
                ring[-1].start()
            across.append(remote(source, spot(step, side, 1), side_send.at[step, side],
                                 side_recv.at[step, side], sibling))
            across[-1].start()
        return ring, across

    ring, copies = send(0)
    for number, view in enumerate(views):
        for hop in (2, 1, 3):
            other = (chip + hop) % CHIPS
            source, target = view(sources[number], targets[number], other, chip)
            copies.append(remote(source, target, send_sem.at[number, hop],
                                 recv_sem.at[number, hop], base + other * CORES))
            copies[-1].start()
    for number, view in enumerate(views):
        source, target = view(sources[number], targets[number], chip, chip)
        copies.append(pltpu.make_async_copy(source, target, local_sem.at[number]))
        copies[-1].start()
    for side in range(2):
        copies.append(pltpu.make_async_copy(
            blocks.at[side], spot(0, side, 0), local_sem.at[count + side]))
        copies[-1].start()
    for step in range(1, steps + 1):
        for copy in ring:
            copy.wait()
        ring, across = send(step)
        copies += across
    for copy in copies:
        copy.wait()


def ring_exchange(blocks, steps, views, sources, shapes, collective_id):
    count = len(views)
    _, depth, width = blocks.shape
    dma = pltpu.SemaphoreType.DMA
    anywhere = pl.BlockSpec(memory_space=pl.ANY)
    return pl.pallas_call(
        functools.partial(ring_kernel, views, steps),
        out_shape=[jax.ShapeDtypeStruct((depth, 4 * width), blocks.dtype)] * (steps + 1) + list(shapes),
        in_specs=[anywhere] * (count + 1),
        out_specs=[anywhere] * (count + steps + 1),
        scratch_shapes=[dma((count, CHIPS)), dma((count, CHIPS)),
                        dma((steps + 1, 2)), dma((steps + 1, 2)),
                        dma((steps + 1, 2)), dma((steps + 1, 2)), dma((count + 2,))],
        compiler_params=pltpu.CompilerParams(
            collective_id=collective_id, has_side_effects=True
        ),
        cost_estimate=pl.CostEstimate(flops=0, bytes_accessed=350_000_000, transcendentals=0),
    )(blocks, *sources)


def to_arrival(info, x_ref, y_ref):
    width = x_ref.shape[1] // 4
    core = info[1]
    x = [x_ref[:, i * width : (i + 1) * width] for i in range(4)]
    for i, (zero, one) in enumerate(((0, 1), (2, 3), (1, 0), (3, 2))):
        y_ref[:, i * width : (i + 1) * width] = jnp.where(core == 0, x[zero], x[one])


def from_arrival(info, x_ref, y_ref):
    width = x_ref.shape[1] // 4
    core = info[1]
    x = [x_ref[:, i * width : (i + 1) * width] for i in range(4)]
    for i, (zero, one) in enumerate(((0, 2), (2, 0), (1, 3), (3, 1))):
        y_ref[:, i * width : (i + 1) * width] = jnp.where(core == 0, x[zero], x[one])


def finish_block(info, x_ref, adapter_ref, scale_ref, y_ref, base_ref):
    from_arrival(info, x_ref, base_ref)
    y_ref[...] = ((base_ref[...] + adapter_ref[...]) * scale_ref[...]).astype(y_ref.dtype)


def reorder(kernel, arrays, kind, forward, info, planes, scratch=()):
    rows, outputs = arrays[0].shape
    block = outputs // planes // 2

    def there(i, info):
        number, side, plane = i // 2, i % 2, info[0]
        falling = (plane + planes - number) % planes
        rising = (plane + number) % planes if forward else (number + planes - plane) % planes
        return 0, jnp.where(side == 0, falling, rising) * 2 + side

    def here(i, info):
        return 0, i

    specs = [pl.BlockSpec((rows, block), there)]
    specs += [pl.BlockSpec((a.shape[0], block), here) for a in arrays[1:]]
    return pl.pallas_call(
        kernel,
        out_shape=jax.ShapeDtypeStruct((rows, outputs), kind),
        grid_spec=pltpu.PrefetchScalarGridSpec(
            num_scalar_prefetch=1,
            grid=(planes * 2,),
            in_specs=specs,
            out_specs=pl.BlockSpec((rows, block), here),
            scratch_shapes=list(scratch),
        ),
    )(info, *arrays)


def rows_to_columns(depth):
    def view(source, target, other, chip):
        rows = source.shape[0]
        return (
            source.at[:, pl.ds(pl.multiple_of(other * depth, 128), depth)],
            target.at[pl.ds(pl.multiple_of(chip * rows, 128), rows), :],
        )
    return view


def columns_to_rows(rows, depth):
    def view(source, target, other, chip):
        return (
            source.at[pl.ds(pl.multiple_of(other * rows, 128), rows), :],
            target.at[:, pl.ds(pl.multiple_of(chip * depth, 128), depth)],
        )
    return view


def whole_rows(source, target, other, chip):
    rows = source.shape[0]
    return source, target.at[pl.ds(pl.multiple_of(chip * rows, 128), rows), :]


def rows_to_slots(rows):
    def view(source, target, other, chip):
        return source.at[pl.ds(pl.multiple_of(other * rows, 128), rows), :], target.at[chip]
    return view


def frozen_view(depth, width):
    def view(source, target, other, chip):
        return (
            source.at[pl.ds(pl.multiple_of(other * depth, 128), depth), :],
            target.at[chip // 2, :, pl.ds(pl.multiple_of((chip % 2) * width, 128), width)],
        )
    return view


def dot(a, b, contract):
    return lax.dot_general(a, b, ((contract[:1], contract[1:]), ((), ())),
                           preferred_element_type=jnp.float32)


def on_plane(tokens, frozen, down, up, magnitude, cotangent):
    rows, features = tokens.shape
    width = frozen.shape[1]
    outputs = cotangent.shape[1]
    size = lax.axis_size("dp")
    planes = size // PLANE
    depth = features // CHIPS
    block = outputs // planes
    me = lax.axis_index("dp")
    plane, chip, core = place()
    info = jnp.stack([plane, core]).astype(jnp.int32)
    f32, bf16 = jnp.float32, jnp.bfloat16

    own_up = lax.dynamic_slice_in_dim(up, me * width, width, 1)
    combined = frozen.astype(f32) + jnp.dot(down, own_up, preferred_element_type=f32)
    squares = jnp.broadcast_to(jnp.sum(combined * combined, axis=0)[None], (8, width))
    blocks, squares = exchange(
        [frozen_view(depth, width)], [frozen],
        [jax.ShapeDtypeStruct((2, depth, 2 * width), bf16)], 1, "gather", squares,
    )
    rank_act = jnp.dot(tokens, down, preferred_element_type=f32).astype(bf16)
    steps = 1
    *weights, tokens_part, cotangent_part, rank_part = ring_exchange(
        blocks, steps, [rows_to_columns(depth), whole_rows, whole_rows],
        [tokens, reorder(to_arrival, [cotangent], bf16, True, info, planes),
         jnp.pad(rank_act, ((0, 0), (0, 128 - rank_act.shape[1] % 128)))],
        [jax.ShapeDtypeStruct((CHIPS * rows, depth), bf16),
         jax.ShapeDtypeStruct((CHIPS * rows, outputs), bf16),
         jax.ShapeDtypeStruct((CHIPS * rows, 128), bf16)], 2,
    )

    forward = [(i, (i + PLANE) % size) for i in range(size)]
    backward = [((i + PLANE) % size, i) for i in range(size)]
    across = [(i, i - i % CORES + (i + 1) % CORES) for i in range(size)]

    def pass_on(pair):
        return lax.ppermute(pair[0], "dp", forward), lax.ppermute(pair[1], "dp", backward)

    def with_other(pair):
        falling, rising = (lax.ppermute(part, "dp", across) for part in pair)
        return jnp.concatenate([pair[0], falling, pair[1], rising], axis=1)

    arriving = pass_on((weights[steps][:, : 2 * width], weights[steps][:, 4 * width : 6 * width]))

    norm = jnp.sqrt(squares[:, :, 0, :].transpose(1, 0, 2).reshape(outputs) + epsilon)
    scale = magnitude.astype(f32) / norm
    scale_rows = jnp.broadcast_to(scale[None], (8, outputs))
    scale_arrival = reorder(to_arrival, [scale_rows], f32, True, info, planes)[:1]

    adapter = jnp.dot(rank_act, up, preferred_element_type=f32)
    cot_own = cotangent.astype(f32)
    factor = 1.0 / math.sqrt(rows * size)

    grad_part = (cotangent_part.astype(f32) * scale_arrival).astype(bf16)
    up_arrival = reorder(to_arrival, [up], bf16, True, info, planes)
    back_part = dot(grad_part, up_arrival, (1, 1)).astype(bf16)
    down_rows = lax.dynamic_slice_in_dim(down, chip * depth, depth, 0)
    gradient = dot(back_part, down_rows, (1, 1))

    rank = up.shape[0]
    down_part = dot(back_part, tokens_part, (0, 0))
    up_part = dot(rank_part, grad_part, (0, 0))[:rank]
    up_part = reorder(from_arrival, [up_part], f32, False, info, planes)
    up_part = lax.dynamic_slice_in_dim(up_part, chip * (outputs // CHIPS), outputs // CHIPS, 1)
    terms = jnp.concatenate([down_part, up_part], axis=1)
    terms = terms.reshape(CORES, planes, rank // (CORES * planes), terms.shape[1])

    partial, sums = [], []

    def apply(step, weight, gradient):
        columns = slice(step * block, (step + 1) * block)
        out = dot(tokens_part, weight, (1, 0))
        gradient = gradient + dot(grad_part[:, columns], weight, (1, 1))
        sums.append(jnp.sum(cotangent_part[:, columns].astype(f32) * out, axis=0))
        partial.append(out.astype(bf16))
        return gradient

    for step in range(steps + 1):
        gradient = lax.optimization_barrier(apply(step, weights[step], gradient))
    early = jnp.concatenate(partial, axis=1)
    arriving, gradient, early, sums, terms = lax.optimization_barrier(
        (arriving, gradient, early, sums, terms)
    )
    for step in range(steps + 1, planes):
        pair = arriving
        if step < planes - 1:
            arriving = pass_on(pair)
        gradient = apply(step, with_other(pair), gradient)
        if step == steps + 1:
            (early_slots,) = exchange(
                [rows_to_slots(rows)], [early],
                [jax.ShapeDtypeStruct((CHIPS, rows, early.shape[1]), bf16)], 3,
            )
        if step < planes - 1:
            arriving, gradient, early_slots, partial, sums = lax.optimization_barrier(
                (arriving, gradient, early_slots, partial, sums)
            )
    late = jnp.concatenate(partial[steps + 1 :], axis=1)
    sums = jnp.broadcast_to(jnp.concatenate(sums)[None], (8, outputs))
    sums = reorder(from_arrival, [sums], f32, False, info, planes)[0]
    sums = (sums + jnp.sum(cot_own * adapter, axis=0)) / norm
    late_slots, input_gradient, grad_magnitude, totals = exchange(
        [rows_to_slots(rows), columns_to_rows(rows, depth)], [late, gradient.astype(bf16)],
        [jax.ShapeDtypeStruct((CHIPS, rows, late.shape[1]), bf16),
         jax.ShapeDtypeStruct((rows, features), bf16)], 4,
        "sum", sums.reshape(outputs // 128, 128), terms,
    )
    totals = totals.transpose(0, 2, 3, 1, 4) * factor
    grad_down = totals[..., :depth].reshape(rank, features).T
    grad_up = totals[..., depth:].reshape(rank, outputs)
    grad_magnitude = grad_magnitude.reshape(outputs)
    base = jnp.concatenate(
        [jnp.sum(early_slots.astype(f32), axis=0), jnp.sum(late_slots.astype(f32), axis=0)], axis=1
    )
    output = reorder(finish_block, [base, adapter, scale[None]], bf16, False, info, planes,
                     [pltpu.VMEM((rows, block // 2), f32)])
    return (output, input_gradient, grad_down, grad_up, grad_magnitude * factor)


def on_device(tokens, frozen_matrix, adapter_down_factor, adapter_up_factor, magnitude, cotangent):
    tok_rows = tokens.shape[0]
    local_portion = adapter_up_factor.shape[1]
    gathered_up_factor, full_magnitude = (
        lax.all_gather(adapter_up_factor, "tensor", axis=1, tiled=True),
        lax.all_gather(magnitude, "tensor", axis=0, tiled=True),
    )
    rank_partial = jnp.dot(tokens, adapter_down_factor, preferred_element_type=jnp.float32)
    rank_activation = lax.psum(rank_partial, "tensor").astype(jnp.bfloat16)
    piece = lax.all_gather(frozen_matrix, "dp", axis=1, tiled=True)
    result = jnp.dot(tokens, piece, preferred_element_type=jnp.float32)
    combined_output = piece.astype(jnp.float32) + jnp.dot(
        adapter_down_factor, gathered_up_factor, preferred_element_type=jnp.float32
    )
    squares = jnp.sum(combined_output * combined_output, axis=0)
    square_part = squares
    squares = lax.psum(square_part, "tensor")
    norm = jnp.sqrt(squares + epsilon)
    scale = full_magnitude.astype(jnp.float32) / norm
    frozen_output = lax.psum_scatter(result, "tensor", scatter_dimension=1, tiled=True)
    shard_start = lax.axis_index("tensor") * local_portion
    merged_weight = frozen_output + jnp.dot(
        rank_activation, adapter_up_factor, preferred_element_type=jnp.float32
    )
    own_scale = lax.dynamic_slice_in_dim(scale, shard_start, local_portion, 0)
    own_norm_vals = lax.dynamic_slice_in_dim(norm, shard_start, local_portion, 0)
    output = (merged_weight * own_scale).astype(jnp.bfloat16)
    rescaled_gradient = (cotangent.astype(jnp.float32) * scale).astype(jnp.bfloat16)
    rank_gradient = jnp.dot(
        rescaled_gradient, gathered_up_factor.T, preferred_element_type=jnp.float32
    ).astype(jnp.bfloat16)
    gradient_running_total = lax.dot_general(
        rescaled_gradient,
        lax.all_gather(frozen_matrix, "dp", axis=1, tiled=True),
        (((1,), (1,)), ((), ())),
        preferred_element_type=jnp.float32,
    )
    input_gradient = (
        gradient_running_total
        + jnp.dot(rank_gradient, adapter_down_factor.T, preferred_element_type=jnp.float32)
    ).astype(jnp.bfloat16)
    own_grad = lax.dynamic_slice_in_dim(rescaled_gradient, shard_start, local_portion, 1)
    own_cotangent = lax.dynamic_slice_in_dim(cotangent, shard_start, local_portion, 1).astype(
        jnp.float32
    )
    down_part = lax.dot_general(
        tokens, rank_gradient, (((0,), (0,)), ((), ())), preferred_element_type=jnp.float32
    )
    up_part = lax.dot_general(
        rank_activation, own_grad, (((0,), (0,)), ((), ())), preferred_element_type=jnp.float32
    )
    magnitude_part = jnp.sum(own_cotangent * merged_weight / own_norm_vals, axis=0)
    grad_down, grad_up, grad_magnitude = lax.psum((down_part, up_part, magnitude_part), "dp")
    factor = 1.0 / math.sqrt(tok_rows * lax.axis_size("dp"))
    return (output, input_gradient, grad_down * factor, grad_up * factor, grad_magnitude * factor)


def solution(mesh):
    planes = mesh.shape["dp"] // PLANE
    in_planes = mesh.shape["tensor"] == 1 and mesh.shape["dp"] == PLANE * planes and planes == 4
    return jax.shard_map(
        on_plane if in_planes else on_device,
        mesh=mesh,
        in_specs=(
            P("dp", "tensor"),
            P("tensor", "dp"),
            P("tensor", None),
            P(None, "tensor"),
            P("tensor"),
            P("dp", None),
        ),
        out_specs=(
            P("dp", "tensor"),
            P("dp", "tensor"),
            P("tensor", None),
            P(None, "tensor"),
            P("tensor"),
        ),
        check_vma=False,
    )
```

```python
import functools
import math

import jax
import jax.numpy as jnp
from jax import lax
from jax.experimental import pallas as pl
from jax.experimental.pallas import tpu as pltpu
from jax.sharding import PartitionSpec as P

epsilon = 1e-06

CHIPS = 4
CORES = 2
PLANE = CHIPS * CORES


def place():
    me = lax.axis_index("dp")
    return me // PLANE, (me % PLANE) // CORES, me % CORES


def exchange_kernel(views, vector, *refs):
    count = len(views)
    ends = count + (vector is not None)
    if vector == "sum":
        ends += 1
    sources, targets = refs[:count], refs[ends : ends + count]
    small_in, small_out = refs[count], refs[ends + count]
    terms, totals = refs[ends - 1], refs[2 * ends - 1]
    scratch = refs[2 * ends :]
    send_sem, recv_sem, local_sem = scratch[:3]
    me = lax.axis_index("dp")
    planes = lax.axis_size("dp") // PLANE
    plane, chip, core = place()
    spot = me % PLANE
    base = me - chip * CORES
    sibling = me - core + (core + 1) % CORES

    def remote(source, target, send, recv, device):
        return pltpu.make_async_remote_copy(
            src_ref=source, dst_ref=target, send_sem=send, recv_sem=recv,
            device_id={"dp": device}, device_id_type=pl.DeviceIdType.MESH,
        )

    if vector is None:
        partners = [base + ((chip + hop) % CHIPS) * CORES for hop in range(1, CHIPS)]
    else:
        above = [(plane + hop) % planes * PLANE + spot for hop in range(1, planes)]
        beside = [plane * PLANE + (spot + hop) % PLANE for hop in range(1, PLANE)]
        partners = above + beside
        group = {}
        for turn in range(CORES):
            for hop in range(planes):
                if turn + hop > 0:
                    group[turn, hop] = (
                        (plane + hop) % planes * PLANE + chip * CORES + (core + turn) % CORES
                    )
        if vector == "sum":
            partners = partners + [group[1, hop] for hop in range(1, planes)]
    barrier = pltpu.get_barrier_semaphore()
    for device in partners:
        pl.semaphore_signal(
            barrier, inc=1, device_id={"dp": device}, device_id_type=pl.DeviceIdType.MESH
        )
    pl.semaphore_wait(barrier, len(partners))

    line = []
    if vector is not None:
        line_send, line_recv, flat_send, flat_recv = scratch[3:7]
        if vector == "gather":
            own = small_out.at[spot, plane]
            keep = pltpu.make_async_copy(small_in, own, local_sem.at[count])
            keep.start()
            start = small_in
        else:
            line_sum, flat_sum, parts, total, part_send, part_recv, total_send, total_recv = scratch[7:]
            mine = parts.at[core, plane]
            keep = pltpu.make_async_copy(terms.at[core, plane], mine, local_sem.at[count])
            keep.start()
            shares = []
            for (turn, hop), device in group.items():
                theirs = terms.at[(core + turn) % CORES, (plane + hop) % planes]
                shares.append(remote(theirs, mine, part_send.at[turn, hop],
                                     part_recv.at[turn, hop], device))
                shares[-1].start()
            own = line_sum.at[plane]
            own[...] = small_in[...]
            start = own
        for hop, device in enumerate(above):
            line.append(remote(start, own, line_send.at[hop], line_recv.at[hop], device))
            line[-1].start()
    copies = []
    for number, view in enumerate(views):
        for hop in (2, 1, 3):
            other = (chip + hop) % CHIPS
            source, target = view(sources[number], targets[number], other, chip)
            copies.append(remote(source, target, send_sem.at[number, hop],
                                 recv_sem.at[number, hop], base + other * CORES))
            copies[-1].start()
    for number, view in enumerate(views):
        source, target = view(sources[number], targets[number], chip, chip)
        copies.append(pltpu.make_async_copy(source, target, local_sem.at[number]))
        copies[-1].start()
    if vector is not None:
        for copy in line:
            copy.wait()
        if vector == "gather":
            keep.wait()
            block = small_out.at[spot]
        else:
            block = flat_sum.at[spot]
            block[...] = functools.reduce(lambda x, y: x + y, [line_sum[i] for i in range(planes)])
        for hop, device in enumerate(beside):
            copies.append(remote(block, block, flat_send.at[hop], flat_recv.at[hop], device))
            copies[-1].start()
    if vector == "sum":
        for copy in shares:
            copy.wait()
        keep.wait()
        total[...] = functools.reduce(
            lambda x, y: x + y, [parts[k, z] for k in range(CORES) for z in range(planes)]
        )
        place_of = totals.at[core, chip, plane]
        keep = pltpu.make_async_copy(total, place_of, local_sem.at[count])
        keep.start()
        stage = [remote(total, place_of, total_send.at[0, hop], total_recv.at[0, hop], device)
                 for hop, device in enumerate(above)]
        for copy in stage:
            copy.start()
        for copy in stage:
            copy.wait()
        keep.wait()
        column = totals.at[core, chip]
        stage = [remote(column, column, total_send.at[1, hop], total_recv.at[1, hop],
                        base + ((chip + hop) % CHIPS) * CORES) for hop in range(1, CHIPS)]
        for copy in stage:
            copy.start()
        for copy in stage:
            copy.wait()
        side = totals.at[core]
        copies.append(remote(side, side, total_send.at[2, 0], total_recv.at[2, 0], sibling))
        copies[-1].start()
    for copy in copies:
        copy.wait()
    if vector == "sum":
        small_out[...] = functools.reduce(lambda x, y: x + y, [flat_sum[i] for i in range(PLANE)])


def exchange(views, sources, shapes, collective_id, vector=None, small=None, terms=None):
    count = len(views)
    planes = lax.axis_size("dp") // PLANE
    moved = sum(math.prod(s.shape) * s.dtype.itemsize for s in shapes)
    sources, shapes = list(sources), list(shapes)
    specs = [pl.BlockSpec(memory_space=pl.ANY)] * count
    dma = pltpu.SemaphoreType.DMA
    scratch = [dma((count, CHIPS)), dma((count, CHIPS)), dma((count + 1,))]
    if vector is not None:
        sources.append(small)
        scratch += [dma((planes,)), dma((planes,)), dma((PLANE,)), dma((PLANE,))]
        if vector == "gather":
            specs = specs + [pl.BlockSpec(memory_space=pl.ANY)]
            shapes.append(jax.ShapeDtypeStruct((PLANE, planes) + small.shape, small.dtype))
        else:
            specs = specs + [pl.BlockSpec(memory_space=pltpu.VMEM)]
            shapes.append(jax.ShapeDtypeStruct(small.shape, small.dtype))
            scratch += [pltpu.VMEM((planes,) + small.shape, small.dtype),
                        pltpu.VMEM((PLANE,) + small.shape, small.dtype)]
            sources.append(terms)
            specs = specs + [pl.BlockSpec(memory_space=pl.ANY)]
            piece = terms.shape[2:]
            shapes.append(jax.ShapeDtypeStruct((CORES, CHIPS, planes) + piece, terms.dtype))
            scratch += [pltpu.VMEM(terms.shape, terms.dtype), pltpu.VMEM(piece, terms.dtype),
                        dma((CORES, planes)), dma((CORES, planes)), dma((3, 4)), dma((3, 4))]
    return pl.pallas_call(
        functools.partial(exchange_kernel, views, vector),
        out_shape=shapes,
        in_specs=specs,
        out_specs=specs,
        scratch_shapes=scratch,
        compiler_params=pltpu.CompilerParams(
            collective_id=collective_id, has_side_effects=True
        ),
        cost_estimate=pl.CostEstimate(flops=0, bytes_accessed=40 * moved, transcendentals=0),
    )(*sources)


def to_arrival(info, x_ref, y_ref):
    width = x_ref.shape[1] // 4
    core = info[1]
    x = [x_ref[:, i * width : (i + 1) * width] for i in range(4)]
    for i, (zero, one) in enumerate(((0, 1), (2, 3), (1, 0), (3, 2))):
        y_ref[:, i * width : (i + 1) * width] = jnp.where(core == 0, x[zero], x[one])


def from_arrival(info, x_ref, y_ref):
    width = x_ref.shape[1] // 4
    core = info[1]
    x = [x_ref[:, i * width : (i + 1) * width] for i in range(4)]
    for i, (zero, one) in enumerate(((0, 2), (2, 0), (1, 3), (3, 1))):
        y_ref[:, i * width : (i + 1) * width] = jnp.where(core == 0, x[zero], x[one])


def finish_block(info, x_ref, adapter_ref, scale_ref, y_ref, base_ref):
    from_arrival(info, x_ref, base_ref)
    y_ref[...] = ((base_ref[...] + adapter_ref[...]) * scale_ref[...]).astype(y_ref.dtype)


def reorder(kernel, arrays, kind, forward, info, planes, scratch=()):
    rows, outputs = arrays[0].shape
    block = outputs // planes // 2

    def there(i, info):
        number, side, plane = i // 2, i % 2, info[0]
        falling = (plane + planes - number) % planes
        rising = (plane + number) % planes if forward else (number + planes - plane) % planes
        return 0, jnp.where(side == 0, falling, rising) * 2 + side

    def here(i, info):
        return 0, i

    specs = [pl.BlockSpec((rows, block), there)]
    specs += [pl.BlockSpec((a.shape[0], block), here) for a in arrays[1:]]
    return pl.pallas_call(
        kernel,
        out_shape=jax.ShapeDtypeStruct((rows, outputs), kind),
        grid_spec=pltpu.PrefetchScalarGridSpec(
            num_scalar_prefetch=1,
            grid=(planes * 2,),
            in_specs=specs,
            out_specs=pl.BlockSpec((rows, block), here),
            scratch_shapes=list(scratch),
        ),
    )(info, *arrays)


def rows_to_columns(depth):
    def view(source, target, other, chip):
        rows = source.shape[0]
        return (
            source.at[:, pl.ds(pl.multiple_of(other * depth, 128), depth)],
            target.at[pl.ds(pl.multiple_of(chip * rows, 128), rows), :],
        )
    return view


def columns_to_rows(rows, depth):
    def view(source, target, other, chip):
        return (
            source.at[pl.ds(pl.multiple_of(other * rows, 128), rows), :],
            target.at[:, pl.ds(pl.multiple_of(chip * depth, 128), depth)],
        )
    return view


def whole_rows(source, target, other, chip):
    rows = source.shape[0]
    return source, target.at[pl.ds(pl.multiple_of(chip * rows, 128), rows), :]


def rows_to_slots(rows):
    def view(source, target, other, chip):
        return source.at[pl.ds(pl.multiple_of(other * rows, 128), rows), :], target.at[chip]
    return view


def frozen_view(depth, width):
    def view(source, target, other, chip):
        return (
            source.at[pl.ds(pl.multiple_of(other * depth, 128), depth), :],
            target.at[chip // 2, :, pl.ds(pl.multiple_of((chip % 2) * width, 128), width)],
        )
    return view


def dot(a, b, contract):
    return lax.dot_general(a, b, ((contract[:1], contract[1:]), ((), ())),
                           preferred_element_type=jnp.float32)


def on_plane(tokens, frozen, down, up, magnitude, cotangent):
    rows, features = tokens.shape
    width = frozen.shape[1]
    outputs = cotangent.shape[1]
    size = lax.axis_size("dp")
    planes = size // PLANE
    depth = features // CHIPS
    block = outputs // planes
    me = lax.axis_index("dp")
    plane, chip, core = place()
    info = jnp.stack([plane, core]).astype(jnp.int32)
    f32, bf16 = jnp.float32, jnp.bfloat16

    own_up = lax.dynamic_slice_in_dim(up, me * width, width, 1)
    combined = frozen.astype(f32) + jnp.dot(down, own_up, preferred_element_type=f32)
    squares = jnp.broadcast_to(jnp.sum(combined * combined, axis=0)[None], (8, width))
    blocks, squares = exchange(
        [frozen_view(depth, width)], [frozen],
        [jax.ShapeDtypeStruct((2, depth, 2 * width), bf16)], 1, "gather", squares,
    )
    forward = [(i, (i + PLANE) % size) for i in range(size)]
    backward = [((i + PLANE) % size, i) for i in range(size)]
    across = [(i, i - i % CORES + (i + 1) % CORES) for i in range(size)]

    def pass_on(pair):
        return lax.ppermute(pair[0], "dp", forward), lax.ppermute(pair[1], "dp", backward)

    def with_other(pair):
        falling, rising = (lax.ppermute(part, "dp", across) for part in pair)
        return jnp.concatenate([pair[0], falling, pair[1], rising], axis=1)

    rank_act = jnp.dot(tokens, down, preferred_element_type=f32).astype(bf16)
    blocks, tokens, cotangent, squares = lax.optimization_barrier(
        (blocks, tokens, cotangent, squares)
    )
    own = (blocks[0], blocks[1])
    arriving = pass_on(own)
    own_weight = with_other(own)
    tokens_part, cotangent_part, rank_part = exchange(
        [rows_to_columns(depth), whole_rows, whole_rows],
        [tokens, reorder(to_arrival, [cotangent], bf16, True, info, planes),
         jnp.pad(rank_act, ((0, 0), (0, 128 - rank_act.shape[1] % 128)))],
        [jax.ShapeDtypeStruct((CHIPS * rows, depth), bf16),
         jax.ShapeDtypeStruct((CHIPS * rows, outputs), bf16),
         jax.ShapeDtypeStruct((CHIPS * rows, 128), bf16)], 2,
    )
    arriving, own_weight, tokens_part, cotangent_part, rank_part = lax.optimization_barrier(
        (arriving, own_weight, tokens_part, cotangent_part, rank_part)
    )
    steps = 1
    pair, arriving = arriving, pass_on(arriving)
    weights = [own_weight, with_other(pair)]

    norm = jnp.sqrt(squares[:, :, 0, :].transpose(1, 0, 2).reshape(outputs) + epsilon)
    scale = magnitude.astype(f32) / norm
    scale_rows = jnp.broadcast_to(scale[None], (8, outputs))
    scale_arrival = reorder(to_arrival, [scale_rows], f32, True, info, planes)[:1]

    adapter = jnp.dot(rank_act, up, preferred_element_type=f32)
    cot_own = cotangent.astype(f32)
    factor = 1.0 / math.sqrt(rows * size)

    grad_part = (cotangent_part.astype(f32) * scale_arrival).astype(bf16)
    up_arrival = reorder(to_arrival, [up], bf16, True, info, planes)
    back_part = dot(grad_part, up_arrival, (1, 1)).astype(bf16)
    down_rows = lax.dynamic_slice_in_dim(down, chip * depth, depth, 0)
    gradient = dot(back_part, down_rows, (1, 1))

    rank = up.shape[0]
    down_part = dot(back_part, tokens_part, (0, 0))
    up_part = dot(rank_part, grad_part, (0, 0))[:rank]
    up_part = reorder(from_arrival, [up_part], f32, False, info, planes)
    up_part = lax.dynamic_slice_in_dim(up_part, chip * (outputs // CHIPS), outputs // CHIPS, 1)
    terms = jnp.concatenate([down_part, up_part], axis=1)
    terms = terms.reshape(CORES, planes, rank // (CORES * planes), terms.shape[1])

    partial, sums = [], []

    def apply(step, weight, gradient):
        columns = slice(step * block, (step + 1) * block)
        out = dot(tokens_part, weight, (1, 0))
        gradient = gradient + dot(grad_part[:, columns], weight, (1, 1))
        sums.append(jnp.sum(cotangent_part[:, columns].astype(f32) * out, axis=0))
        partial.append(out.astype(bf16))
        return gradient

    for step in range(steps + 1):
        gradient = lax.optimization_barrier(apply(step, weights[step], gradient))
    early = jnp.concatenate(partial, axis=1)
    arriving, gradient, early, sums, terms = lax.optimization_barrier(
        (arriving, gradient, early, sums, terms)
    )
    for step in range(steps + 1, planes):
        pair = arriving
        if step < planes - 1:
            arriving = pass_on(pair)
        gradient = apply(step, with_other(pair), gradient)
        if step == steps + 1:
            (early_slots,) = exchange(
                [rows_to_slots(rows)], [early],
                [jax.ShapeDtypeStruct((CHIPS, rows, early.shape[1]), bf16)], 3,
            )
        if step < planes - 1:
            arriving, gradient, early_slots, partial, sums = lax.optimization_barrier(
                (arriving, gradient, early_slots, partial, sums)
            )
    late = jnp.concatenate(partial[steps + 1 :], axis=1)
    sums = jnp.broadcast_to(jnp.concatenate(sums)[None], (8, outputs))
    sums = reorder(from_arrival, [sums], f32, False, info, planes)[0]
    sums = (sums + jnp.sum(cot_own * adapter, axis=0)) / norm
    late_slots, input_gradient, grad_magnitude, totals = exchange(
        [rows_to_slots(rows), columns_to_rows(rows, depth)], [late, gradient.astype(bf16)],
        [jax.ShapeDtypeStruct((CHIPS, rows, late.shape[1]), bf16),
         jax.ShapeDtypeStruct((rows, features), bf16)], 4,
        "sum", sums.reshape(outputs // 128, 128), terms,
    )
    totals = totals.transpose(0, 2, 3, 1, 4) * factor
    grad_down = totals[..., :depth].reshape(rank, features).T
    grad_up = totals[..., depth:].reshape(rank, outputs)
    grad_magnitude = grad_magnitude.reshape(outputs)
    base = jnp.concatenate(
        [jnp.sum(early_slots.astype(f32), axis=0), jnp.sum(late_slots.astype(f32), axis=0)], axis=1
    )
    output = reorder(finish_block, [base, adapter, scale[None]], bf16, False, info, planes,
                     [pltpu.VMEM((rows, block // 2), f32)])
    return (output, input_gradient, grad_down, grad_up, grad_magnitude * factor)


def on_device(tokens, frozen_matrix, adapter_down_factor, adapter_up_factor, magnitude, cotangent):
    tok_rows = tokens.shape[0]
    local_portion = adapter_up_factor.shape[1]
    gathered_up_factor, full_magnitude = (
        lax.all_gather(adapter_up_factor, "tensor", axis=1, tiled=True),
        lax.all_gather(magnitude, "tensor", axis=0, tiled=True),
    )
    rank_partial = jnp.dot(tokens, adapter_down_factor, preferred_element_type=jnp.float32)
    rank_activation = lax.psum(rank_partial, "tensor").astype(jnp.bfloat16)
    piece = lax.all_gather(frozen_matrix, "dp", axis=1, tiled=True)
    result = jnp.dot(tokens, piece, preferred_element_type=jnp.float32)
    combined_output = piece.astype(jnp.float32) + jnp.dot(
        adapter_down_factor, gathered_up_factor, preferred_element_type=jnp.float32
    )
    squares = jnp.sum(combined_output * combined_output, axis=0)
    square_part = squares
    squares = lax.psum(square_part, "tensor")
    norm = jnp.sqrt(squares + epsilon)
    scale = full_magnitude.astype(jnp.float32) / norm
    frozen_output = lax.psum_scatter(result, "tensor", scatter_dimension=1, tiled=True)
    shard_start = lax.axis_index("tensor") * local_portion
    merged_weight = frozen_output + jnp.dot(
        rank_activation, adapter_up_factor, preferred_element_type=jnp.float32
    )
    own_scale = lax.dynamic_slice_in_dim(scale, shard_start, local_portion, 0)
    own_norm_vals = lax.dynamic_slice_in_dim(norm, shard_start, local_portion, 0)
    output = (merged_weight * own_scale).astype(jnp.bfloat16)
    rescaled_gradient = (cotangent.astype(jnp.float32) * scale).astype(jnp.bfloat16)
    rank_gradient = jnp.dot(
        rescaled_gradient, gathered_up_factor.T, preferred_element_type=jnp.float32
    ).astype(jnp.bfloat16)
    gradient_running_total = lax.dot_general(
        rescaled_gradient,
        lax.all_gather(frozen_matrix, "dp", axis=1, tiled=True),
        (((1,), (1,)), ((), ())),
        preferred_element_type=jnp.float32,
    )
    input_gradient = (
        gradient_running_total
        + jnp.dot(rank_gradient, adapter_down_factor.T, preferred_element_type=jnp.float32)
    ).astype(jnp.bfloat16)
    own_grad = lax.dynamic_slice_in_dim(rescaled_gradient, shard_start, local_portion, 1)
    own_cotangent = lax.dynamic_slice_in_dim(cotangent, shard_start, local_portion, 1).astype(
        jnp.float32
    )
    down_part = lax.dot_general(
        tokens, rank_gradient, (((0,), (0,)), ((), ())), preferred_element_type=jnp.float32
    )
    up_part = lax.dot_general(
        rank_activation, own_grad, (((0,), (0,)), ((), ())), preferred_element_type=jnp.float32
    )
    magnitude_part = jnp.sum(own_cotangent * merged_weight / own_norm_vals, axis=0)
    grad_down, grad_up, grad_magnitude = lax.psum((down_part, up_part, magnitude_part), "dp")
    factor = 1.0 / math.sqrt(tok_rows * lax.axis_size("dp"))
    return (output, input_gradient, grad_down * factor, grad_up * factor, grad_magnitude * factor)


def solution(mesh):
    planes = mesh.shape["dp"] // PLANE
    in_planes = mesh.shape["tensor"] == 1 and mesh.shape["dp"] == PLANE * planes and planes == 4
    return jax.shard_map(
        on_plane if in_planes else on_device,
        mesh=mesh,
        in_specs=(
            P("dp", "tensor"),
            P("tensor", "dp"),
            P("tensor", None),
            P(None, "tensor"),
            P("tensor"),
            P("dp", None),
        ),
        out_specs=(
            P("dp", "tensor"),
            P("dp", "tensor"),
            P("tensor", None),
            P(None, "tensor"),
            P("tensor"),
        ),
        check_vma=False,
    )
```
